128 devices in a mesh: dp: 16 (over z_hi, x, core), head: 8 (over y, z_lo).
Axes of the slice: x: 4, y: 4, z: 4 (z_hi: 2, z_lo: 2; z = z_hi * 2 + z_lo), core: 2. Of those that a mesh axis runs over, the one named last changes fastest.
Arguments:
- tokens: bfloat16 [16384, 8192], P('dp'), may hold values from -64 to 64
- w_query: bfloat16 [8192, 8192], P('dp', 'head'), may hold values from -0.0625 to 0.0625
- key_weight: bfloat16 [8192, 1024], P('dp', 'head'), may hold values from -0.0625 to 0.0625
- value_weight: bfloat16 [8192, 1024], P('dp', 'head'), may hold values from -0.0625 to 0.0625
- segment_ids: int32 [16384], P('dp'), may hold values from 0 to 27, as said below
Outputs:
- attended: bfloat16 [16384, 8192], P('dp', 'head')
The draws below stay inside these ranges and needn't reach their ends.
Inputs may be any that keep to these rules, and one draw needn't show every extreme that they name: `segment_ids`: within each sequence of 1024 tokens the numbers start at 0 and never fall.
All inputs are finite; a program needn't handle non-finite values.
Results may differ from the reference program's by a relative error of at most 0.01.
The reference program's roundings to bfloat16 on the way count: a program that leaves them out, or rounds other values in their place, can miss the bound.
Values may be sent and summed in bfloat16 or wider, within the bound.
A program may use at most 128 MiB of HBM per device.

```python
import jax
import jax.numpy as jnp
from jax import lax

MODEL_WIDTH = 8192
QUERY_HEADS = 64
KEY_VALUE_HEADS = 8
HEAD_SIZE = 128
PACKED_TOKENS = 1024
TOKENS = 16384
N_DP = 16


def draw_tokens(key, part):
    values = jnp.clip(jax.random.normal(key, (TOKENS, MODEL_WIDTH), jnp.float32), -6.0, 6.0)
    return values.astype(jnp.bfloat16)


def draw_segment_ids(key, part):
    first, second = jax.random.split(jax.random.fold_in(key, 11))
    level = jax.random.randint(first, (N_DP, 1), 0, 4)
    counts = level * level * level
    cuts = jax.random.randint(second, (N_DP, 27), 1, PACKED_TOKENS)
    active = jnp.arange(27)[None, :] < counts
    positions = jnp.arange(PACKED_TOKENS)
    passed = (cuts[:, None, :] <= positions[None, :, None]) & active[:, None, :]
    ids = jnp.sum(passed.astype(jnp.int32), axis=2).astype(jnp.int32)
    return ids.reshape(TOKENS)


def shard_levels(own_key, extent, cuts, least, top_value):
    def one(axis_at, blocks):
        heights = jax.random.uniform(jax.random.fold_in(jax.random.fold_in(own_key, 6), axis_at), (blocks,), jnp.float32, least / len(cuts), top_value / len(cuts))
        return jnp.repeat(jnp.exp(heights), extent[axis_at] // blocks).reshape((-1,) + (1,) * (len(extent) - axis_at - 1))

    loudness = one(*cuts[0])
    for cut in cuts[1:]:
        loudness = loudness * one(*cut)
    return loudness


def normal_values(rng, extent, width, most, cuts=(), kind=jnp.bfloat16):
    values = jax.random.normal(rng, extent, jnp.float32) * width
    if len(cuts) > 0:
        values = shard_levels(rng, extent, cuts, -0.22, 0.18) * values
    return jnp.clip(values, min=-most, max=most).astype(kind)


def setup_inputs(seed: int = 0) -> dict:
    seeds = jax.random.split(jax.random.key(seed), 6)
    tokens = draw_tokens(jax.random.fold_in(seeds[5], 71), 0)
    w_query = normal_values(seeds[1], (MODEL_WIDTH, QUERY_HEADS * HEAD_SIZE), MODEL_WIDTH ** -0.5, 0.0625, ((0, 16), (1, 8)))
    key_weight = normal_values(seeds[2], (MODEL_WIDTH, KEY_VALUE_HEADS * HEAD_SIZE), MODEL_WIDTH ** -0.5, 0.0625, ((0, 16), (1, 8)))
    value_weight = normal_values(seeds[3], (MODEL_WIDTH, KEY_VALUE_HEADS * HEAD_SIZE), MODEL_WIDTH ** -0.5, 0.0625, ((0, 16), (1, 8)))
    segment_ids = draw_segment_ids(jax.random.fold_in(seeds[5], 71), 0)
    return {"tokens": tokens, "w_query": w_query, "key_weight": key_weight, "value_weight": value_weight, "segment_ids": segment_ids}


def reference(tokens, w_query, key_weight, value_weight, segment_ids):
    grouped_heads = QUERY_HEADS // KEY_VALUE_HEADS

    def one_sequence(index):
        rows = lax.dynamic_slice_in_dim(tokens, index * PACKED_TOKENS, PACKED_TOKENS, 0)
        segments = lax.dynamic_slice_in_dim(segment_ids, index * PACKED_TOKENS, PACKED_TOKENS, 0)
        query_matrix = jnp.dot(rows, w_query, preferred_element_type=jnp.float32).astype(jnp.bfloat16)
        key = jnp.dot(rows, key_weight, preferred_element_type=jnp.float32).astype(jnp.bfloat16)
        value_matrix = jnp.dot(rows, value_weight, preferred_element_type=jnp.float32).astype(jnp.bfloat16)
        query_matrix = query_matrix.reshape(PACKED_TOKENS, KEY_VALUE_HEADS, grouped_heads, HEAD_SIZE).astype(jnp.float32)
        key = key.reshape(PACKED_TOKENS, KEY_VALUE_HEADS, HEAD_SIZE).astype(jnp.float32)
        value_matrix = value_matrix.reshape(PACKED_TOKENS, KEY_VALUE_HEADS, HEAD_SIZE).astype(jnp.float32)
        positions = jnp.arange(PACKED_TOKENS, dtype=jnp.int32)
        mask = (positions[None, :] <= positions[:, None]) & (segments[None, :] == segments[:, None])
        scores = jnp.einsum('qhgd,khd->hgqk', query_matrix, key) / jnp.sqrt(jnp.float32(HEAD_SIZE))
        scores = jnp.where(mask, scores, jnp.float32(-1e+30))
        highest = lax.optimization_barrier(jnp.max(scores, axis=3, keepdims=True))
        weights = jnp.where(mask, jnp.exp(scores - highest), jnp.float32(0.0))
        denominator = lax.optimization_barrier(jnp.sum(weights, axis=3))
        rounded = lax.optimization_barrier(weights.astype(jnp.bfloat16)).astype(jnp.float32)
        summed = jnp.einsum('hgqk,khd->hgqd', rounded, value_matrix)
        result = summed / denominator[..., None]
        return jnp.transpose(result, (2, 0, 1, 3)).reshape(PACKED_TOKENS, QUERY_HEADS * HEAD_SIZE).astype(jnp.bfloat16)
    outputs = lax.map(one_sequence, jnp.arange(N_DP, dtype=jnp.int32))
    return outputs.reshape(TOKENS, QUERY_HEADS * HEAD_SIZE)
```

```python
import functools
import math

import jax
import jax.numpy as jnp
from jax import lax
from jax.experimental import pallas as pl
from jax.experimental.pallas import tpu as pltpu
from jax.sharding import PartitionSpec as P

MESH = pl.DeviceIdType.MESH
HEAD = 128
PAIR = 2 * HEAD
NEGATIVE = -1e30
EXP2_SCALE = math.log2(math.e) / math.sqrt(HEAD)
LANE = 10
BLOCKS = 8
ROWS_X = 432
TILE = 256


def kernel(tok_hbm, wq_hbm, wk_hbm, wv_hbm, seg_ref, out_hbm,
           tok, w, acc, qkv, bias, outs,
           load_sem, tok_sem, out_sem, send_sem, recv_sem):
    tokens, width = tok.shape
    chunks = w.shape[0]
    rows = wq_hbm.shape[0]
    last = chunks - 1
    half = rows // 2
    me = lax.axis_index("dp")
    head = lax.axis_index("head")
    zh, x, core = me // 8, lax.rem(me // 2, 4), lax.rem(me, 2)

    def device(dz, dx, dc):
        return (lax.rem(zh + dz, 2) * 4 + lax.rem(x + dx, 4)) * 2 + lax.rem(core + dc, 2)

    OWN, XP, XM, X2, ZO, PP, PM, CO = (0, 0), (0, 1), (0, 3), (0, 2), (1, 0), (1, 1), (1, 3), (1, 2)
    ORDER = (OWN, XP, XM, X2, ZO, PP, PM, CO)
    to_left, to_right = (device(0, 3, 0), head), (device(0, 1, 0), head)
    partner, sibling = (device(1, 0, 0), head), (device(0, 0, 1), head)

    def part(c, pos, dc, first, count):
        start = pl.multiple_of(device(pos[0], pos[1], dc) * rows + first, 16)
        return w.at[c, pl.ds(start, count)]

    def send(c, pos, first, count, target, slot):
        ref = part(c, pos, 0, first, count)
        pltpu.make_async_remote_copy(
            src_ref=ref, dst_ref=ref, send_sem=send_sem.at[c, slot], recv_sem=recv_sem.at[c, slot],
            device_id=target, device_id_type=MESH).start()

    def pair(c, pos):
        send(c, pos, 0, rows, sibling, LANE + ORDER.index(pos))

    def wait(c, pos, first, count, slot, dc=0):
        ref = part(c, pos, dc, first, count)
        pltpu.make_async_remote_copy(
            src_ref=ref, dst_ref=ref, send_sem=send_sem.at[c, slot], recv_sem=recv_sem.at[c, slot],
            device_id=sibling, device_id_type=MESH).wait_recv()

    def send_own(c):
        send(c, OWN, 0, rows, to_left, 0)
        send(c, OWN, 0, rows, to_right, 1)
        send(c, OWN, 0, rows, partner, 6)
        pair(c, OWN)

    def take_x(c):
        wait(c, XP, 0, rows, 0)
        wait(c, XM, 0, rows, 1)
        if ROWS_X < rows:
            send(c, XP, ROWS_X, rows - ROWS_X, partner, 8)
            send(c, XM, ROWS_X, rows - ROWS_X, partner, 9)
        pair(c, XP)
        pair(c, XM)

    def send_halves(c):
        send(c, XP, 0, half, to_left, 2)
        send(c, XM, half, half, to_right, 3)

    def take_z(c):
        wait(c, ZO, 0, rows, 6)
        send(c, ZO, 0, ROWS_X, to_left, 4)
        send(c, ZO, 0, ROWS_X, to_right, 5)
        pair(c, ZO)

    def take_halves(c):
        wait(c, X2, 0, half, 2)
        wait(c, X2, half, half, 3)
        send(c, X2, 0, rows, partner, 7)
        pair(c, X2)

    def take_far(c):
        wait(c, PP, 0, ROWS_X, 4)
        wait(c, PM, 0, ROWS_X, 5)
        if ROWS_X < rows:
            wait(c, PP, ROWS_X, rows - ROWS_X, 8)
            wait(c, PM, ROWS_X, rows - ROWS_X, 9)
        pair(c, PP)
        pair(c, PM)

    def take_corner(c):
        wait(c, CO, 0, rows, 7)
        pair(c, CO)

    def take_siblings(c):
        for i, pos in enumerate(ORDER):
            wait(c, pos, 0, rows, LANE + i, dc=1)

    def project(c, pos, first=False):
        start = pl.multiple_of((lax.rem(zh + pos[0], 2) * 4 + lax.rem(x + pos[1], 4)) * 2 * rows, 1024)

        def tile(i, carry):
            at = pl.ds(pl.multiple_of(i * 512, 512), 512)
            part_sum = jnp.dot(tok[at, pl.ds(start, 2 * rows)], w[c, pl.ds(start, 2 * rows)],
                               preferred_element_type=jnp.float32)
            acc[at] = part_sum if first else acc[at] + part_sum
            return carry

        lax.fori_loop(0, tokens // 512, tile, 0)

    def round_chunk(c):
        for h in range(2):
            qkv[c, h] = acc[:, h * HEAD:(h + 1) * HEAD].astype(jnp.bfloat16)

    def attend(c, h):
        for i in range(tokens // TILE):
            n = (i + 1) * TILE
            at = slice(i * TILE, n)
            s = lax.dot_general(qkv[c, h, at], qkv[0, 0, :n], (((1,), (1,)), ((), ())),
                                preferred_element_type=jnp.float32)
            s = s + bias[at, :n]
            p = jnp.exp2((s - jnp.max(s, axis=1, keepdims=True)) * EXP2_SCALE)
            total = jnp.sum(p, axis=1, keepdims=True)
            o = jnp.dot(p.astype(jnp.bfloat16), qkv[0, 1, :n], preferred_element_type=jnp.float32)
            outs[(c - 1) * 2 + h, at] = (o / total).astype(jnp.bfloat16)
        out_copy(c, h).start()

    def out_copy(c, h):
        j = (c - 1) * 2 + h
        return pltpu.make_async_copy(
            outs.at[j], out_hbm.at[:, pl.ds(pl.multiple_of(j * HEAD, HEAD), HEAD)], out_sem.at[j])

    def loads(c):
        at = pl.ds(pl.multiple_of(me * rows, rows), rows)
        if c == 0:
            return [pltpu.make_async_copy(wk_hbm, w.at[0, at, pl.ds(0, HEAD)], load_sem.at[0]),
                    pltpu.make_async_copy(wv_hbm, w.at[0, at, pl.ds(HEAD, HEAD)], load_sem.at[chunks])]
        return [pltpu.make_async_copy(wq_hbm.at[:, pl.ds((c - 1) * PAIR, PAIR)], w.at[c, at], load_sem.at[c])]

    for c in range(chunks):
        for copy in loads(c):
            copy.start()
    tok_copy = pltpu.make_async_copy(tok_hbm, tok, tok_sem)
    tok_copy.start()

    barrier = pltpu.get_barrier_semaphore()
    for target in (to_left, to_right, partner, sibling):
        pl.semaphore_signal(barrier, inc=1, device_id=target, device_id_type=MESH)
    pl.semaphore_wait(barrier, 4)

    for c in range(chunks):
        for copy in loads(c):
            copy.wait()
        if c < 2:
            send_own(c)

    for i in range(tokens // HEAD):
        mine = jnp.transpose(jnp.broadcast_to(seg_ref[i:i + 1, :], (HEAD, HEAD)))
        for j in range((i * HEAD // TILE + 1) * TILE // HEAD):
            ok = mine == jnp.broadcast_to(seg_ref[j:j + 1, :], (HEAD, HEAD))
            t = lax.broadcasted_iota(jnp.int32, (HEAD, HEAD), 0) + i * HEAD
            u = lax.broadcasted_iota(jnp.int32, (HEAD, HEAD), 1) + j * HEAD
            bias[i * HEAD:(i + 1) * HEAD, j * HEAD:(j + 1) * HEAD] = jnp.where(
                jnp.logical_and(ok, u <= t), jnp.float32(0.0), jnp.float32(NEGATIVE))

    take_x(0)
    send_halves(0)
    tok_copy.wait()

    def body(c, carry):
        @pl.when(c < last)
        def _():
            take_x(c + 1)

        take_z(c)

        @pl.when(c > 0)
        def _():
            project(c - 1, OWN, first=True)
            for pos in (XP, XM, X2):
                project(c - 1, pos)

        take_halves(c)

        @pl.when(c < last - 1)
        def _():
            send_own(c + 2)

        @pl.when(c > 0)
        def _():
            for pos in (ZO, PP, PM, CO):
                project(c - 1, pos)
            round_chunk(c - 1)

        take_far(c)

        @pl.when(c < last)
        def _():
            send_halves(c + 1)

        @pl.when(c > 1)
        def _():
            attend(c - 1, 0)

        take_corner(c)

        @pl.when(c > 1)
        def _():
            attend(c - 1, 1)

        take_siblings(c)
        return carry

    lax.fori_loop(0, chunks, body, 0)

    project(last, OWN, first=True)
    for pos in ORDER[1:]:
        project(last, pos)
    round_chunk(last)
    attend(last, 0)
    attend(last, 1)

    def drain(c, carry):
        for slot, (pos, first, count) in enumerate(
                ((OWN, 0, rows), (OWN, 0, rows), (XP, 0, half), (XM, half, half), (ZO, 0, ROWS_X), (ZO, 0, ROWS_X),
                 (OWN, 0, rows), (X2, 0, rows), (XP, ROWS_X, rows - ROWS_X), (XM, ROWS_X, rows - ROWS_X))
                + tuple((pos, 0, rows) for pos in ORDER)):
            if count > 0:
                ref = part(c, pos, 0, first, count)
                pltpu.make_async_remote_copy(
                    src_ref=ref, dst_ref=ref, send_sem=send_sem.at[c, slot], recv_sem=recv_sem.at[c, slot],
                    device_id=sibling, device_id_type=MESH).wait_send()
        return carry

    lax.fori_loop(0, chunks, drain, 0)

    def drain_out(c, carry):
        for h in range(2):
            out_copy(c, h).wait()
        return carry

    lax.fori_loop(1, chunks, drain_out, 0)


def body(tokens, w_query, key_weight, value_weight, segment_ids):
    seq, width = tokens.shape
    rows, columns = w_query.shape
    chunks = columns // PAIR + 1
    heads = columns // HEAD
    any_space = pl.BlockSpec(memory_space=pl.ANY)
    flops = 2 * seq * width * (columns + PAIR)
    return pl.pallas_call(
        kernel,
        out_shape=jax.ShapeDtypeStruct((seq, columns), jnp.bfloat16),
        in_specs=[any_space] * 4 + [pl.BlockSpec(memory_space=pltpu.VMEM)],
        out_specs=any_space,
        scratch_shapes=[
            pltpu.VMEM((seq, width), jnp.bfloat16),
            pltpu.VMEM((chunks, width, PAIR), jnp.bfloat16),
            pltpu.VMEM((seq, PAIR), jnp.float32),
            pltpu.VMEM((chunks, 2, seq, HEAD), jnp.bfloat16),
            pltpu.VMEM((seq, seq), jnp.float32),
            pltpu.VMEM((heads, seq, HEAD), jnp.bfloat16),
            pltpu.SemaphoreType.DMA((chunks + 1,)),
            pltpu.SemaphoreType.DMA,
            pltpu.SemaphoreType.DMA((heads,)),
            pltpu.SemaphoreType.DMA((chunks, LANE + BLOCKS)),
            pltpu.SemaphoreType.DMA((chunks, LANE + BLOCKS)),
        ],
        compiler_params=pltpu.CompilerParams(
            collective_id=0, has_side_effects=True, vmem_limit_bytes=58 * 2**20),
        cost_estimate=pl.CostEstimate(flops=flops, bytes_accessed=40 * 2**20, transcendentals=8 * seq * seq),
    )(tokens, w_query, key_weight, value_weight, segment_ids.reshape(seq // HEAD, HEAD))


def solution(mesh):
    in_specs = (P("dp", None), P("dp", "head"), P("dp", "head"), P("dp", "head"), P("dp"))
    return jax.shard_map(body, mesh=mesh, in_specs=in_specs, out_specs=P("dp", "head"), check_vma=False)
```

```python
import functools
import math

import jax
import jax.numpy as jnp
from jax import lax
from jax.experimental import pallas as pl
from jax.experimental.pallas import tpu as pltpu
from jax.sharding import PartitionSpec as P

MESH = pl.DeviceIdType.MESH
HEAD = 128
PAIR = 2 * HEAD
NEGATIVE = -1e30
EXP2_SCALE = math.log2(math.e) / math.sqrt(HEAD)
LANE = 10
BLOCKS = 8
ROWS_X = 432
TILE = 256

ORDER = (
    ("own", 0), ("own", 1), ("mul", 0, "OWN"), ("own", 2), ("x", 0), ("z", 0), ("mul", 0, "XP"),
    ("mul", 0, "XM"), ("mul", 0, "ZO"), ("x", 1), ("z", 1), ("x", 2), ("z", 2), ("halves", 0),
    ("mul", 0, "X2"), ("far", 0), ("halves", 1), ("far", 1), ("halves", 2), ("corner", 0), ("own", 3),
    ("mul", 0, "CO"), ("take_far", 0), ("mul", 0, "PP"), ("mul", 0, "PM"), ("corner", 1), ("round", 0),
    ("far", 2), ("mul", 1, "OWN"), ("mul", 1, "XP"), ("take_far", 1), ("mul", 1, "XM"), ("mul", 1, "ZO"),
    ("mul", 1, "X2"), ("mul", 1, "CO"), ("mul", 1, "PP"), ("mul", 1, "PM"), ("round", 1), ("attend", 1, 0),
    ("corner", 2), ("own", 4), ("attend", 1, 1), ("attend", 1, 2), ("x", 3), ("attend", 1, 3),
    ("mul", 2, "OWN"), ("mul", 2, "XP"), ("mul", 2, "XM"), ("mul", 2, "ZO"), ("mul", 2, "X2"),
    ("mul", 2, "CO"), ("z", 3), ("take_far", 2), ("mul", 2, "PP"), ("mul", 2, "PM"), ("round", 2),
    ("attend", 2, 0), ("far", 3), ("attend", 2, 1), ("z", 4), ("attend", 2, 2), ("x", 4), ("attend", 2, 3),
    ("mul", 3, "OWN"), ("mul", 3, "XP"), ("mul", 3, "XM"), ("halves", 3), ("mul", 3, "ZO"), ("mul", 3, "X2"),
    ("far", 4), ("take_far", 3), ("corner", 3), ("mul", 3, "PP"), ("halves", 4), ("mul", 3, "PM"),
    ("mul", 3, "CO"), ("round", 3), ("attend", 3, 0), ("attend", 3, 1), ("attend", 3, 2), ("attend", 3, 3),
    ("mul", 4, "OWN"), ("mul", 4, "XP"), ("take_far", 4), ("mul", 4, "XM"), ("mul", 4, "ZO"), ("mul", 4, "X2"),
    ("corner", 4), ("mul", 4, "PP"), ("mul", 4, "PM"), ("mul", 4, "CO"), ("round", 4), ("attend", 4, 0),
    ("attend", 4, 1), ("attend", 4, 2), ("attend", 4, 3),
)


def kernel(tok_hbm, wq_hbm, wk_hbm, wv_hbm, seg_ref, out_hbm,
           tok, w, acc, qkv, bias, outs,
           load_sem, tok_sem, out_sem, send_sem, recv_sem):
    tokens, width = tok.shape
    chunks = w.shape[0]
    rows = wq_hbm.shape[0]
    last = chunks - 1
    half = rows // 2
    me = lax.axis_index("dp")
    head = lax.axis_index("head")
    zh, x, core = me // 8, lax.rem(me // 2, 4), lax.rem(me, 2)

    def device(dz, dx, dc):
        return (lax.rem(zh + dz, 2) * 4 + lax.rem(x + dx, 4)) * 2 + lax.rem(core + dc, 2)

    OWN, XP, XM, X2, ZO, PP, PM, CO = (0, 0), (0, 1), (0, 3), (0, 2), (1, 0), (1, 1), (1, 3), (1, 2)
    ALL = (OWN, XP, XM, X2, ZO, PP, PM, CO)
    BY_NAME = dict(OWN=OWN, XP=XP, XM=XM, X2=X2, ZO=ZO, PP=PP, PM=PM, CO=CO)
    to_left, to_right = (device(0, 3, 0), head), (device(0, 1, 0), head)
    partner, sibling = (device(1, 0, 0), head), (device(0, 0, 1), head)

    def part(c, pos, dc, first, count):
        start = pl.multiple_of(device(pos[0], pos[1], dc) * rows + first, 16)
        return w.at[c, pl.ds(start, count)]

    def send(c, pos, first, count, target, slot):
        ref = part(c, pos, 0, first, count)
        pltpu.make_async_remote_copy(
            src_ref=ref, dst_ref=ref, send_sem=send_sem.at[c, slot], recv_sem=recv_sem.at[c, slot],
            device_id=target, device_id_type=MESH).start()

    def pair(c, pos):
        send(c, pos, 0, rows, sibling, LANE + ALL.index(pos))

    def wait(c, pos, first, count, slot, dc=0):
        ref = part(c, pos, dc, first, count)
        pltpu.make_async_remote_copy(
            src_ref=ref, dst_ref=ref, send_sem=send_sem.at[c, slot], recv_sem=recv_sem.at[c, slot],
            device_id=sibling, device_id_type=MESH).wait_recv()

    def send_own(c):
        send(c, OWN, 0, rows, to_left, 0)
        send(c, OWN, 0, rows, to_right, 1)
        send(c, OWN, 0, rows, partner, 6)
        pair(c, OWN)

    def take_x(c):
        wait(c, XP, 0, rows, 0)
        send(c, XP, 0, half, to_left, 2)
        wait(c, XM, 0, rows, 1)
        send(c, XM, half, half, to_right, 3)
        if ROWS_X < rows:
            send(c, XP, ROWS_X, rows - ROWS_X, partner, 8)
            send(c, XM, ROWS_X, rows - ROWS_X, partner, 9)
        pair(c, XP)
        pair(c, XM)

    def take_z(c):
        wait(c, ZO, 0, rows, 6)
        pair(c, ZO)

    def send_far(c):
        send(c, ZO, 0, ROWS_X, to_left, 4)
        send(c, ZO, 0, ROWS_X, to_right, 5)

    def take_halves(c):
        wait(c, X2, 0, half, 2)
        wait(c, X2, half, half, 3)
        send(c, X2, 0, rows, partner, 7)
        pair(c, X2)

    def take_far(c):
        wait(c, PP, 0, ROWS_X, 4)
        wait(c, PM, 0, ROWS_X, 5)
        if ROWS_X < rows:
            wait(c, PP, ROWS_X, rows - ROWS_X, 8)
            wait(c, PM, ROWS_X, rows - ROWS_X, 9)
        pair(c, PP)
        pair(c, PM)

    def take_corner(c):
        wait(c, CO, 0, rows, 7)
        pair(c, CO)

    started = set()

    def project(c, name):
        pos = BY_NAME[name]
        wait(c, pos, 0, rows, LANE + ALL.index(pos), dc=1)
        start = pl.multiple_of((lax.rem(zh + pos[0], 2) * 4 + lax.rem(x + pos[1], 4)) * 2 * rows, 1024)
        first = c not in started
        started.add(c)
        def go():
            part_sum = jnp.dot(tok[:, pl.ds(start, 2 * rows)], w[c, pl.ds(start, 2 * rows)],
                               preferred_element_type=jnp.float32)
            acc[...] = part_sum if first else acc[...] + part_sum
        pl.when(me >= 0)(go)

    def round_chunk(c):
        def go():
            for h in range(2):
                qkv[c, h] = acc[:, h * HEAD:(h + 1) * HEAD].astype(jnp.bfloat16)
        pl.when(me >= 0)(go)

    def attend(c, i):
        pl.when(me >= 0)(functools.partial(attend_in, c, i))

    def attend_in(c, i):
        n = (i + 1) * TILE
        at = slice(i * TILE, n)
        scores = [lax.dot_general(qkv[c, h, at], qkv[0, 0, :n], (((1,), (1,)), ((), ())),
                                  preferred_element_type=jnp.float32) + bias[at, :n] for h in range(2)]
        weights = [jnp.exp2((s - jnp.max(s, axis=1, keepdims=True)) * EXP2_SCALE) for s in scores]
        for h, p in enumerate(weights):
            total = jnp.sum(p, axis=1, keepdims=True)
            o = jnp.dot(p.astype(jnp.bfloat16), qkv[0, 1, :n], preferred_element_type=jnp.float32)
            outs[(c - 1) * 2 + h, at] = (o / total).astype(jnp.bfloat16)
        if i == tokens // TILE - 1:
            for h in range(2):
                out_copy(c, h).start()

    def out_copy(c, h):
        j = (c - 1) * 2 + h
        return pltpu.make_async_copy(
            outs.at[j], out_hbm.at[:, pl.ds(pl.multiple_of(j * HEAD, HEAD), HEAD)], out_sem.at[j])

    def loads(c):
        at = pl.ds(pl.multiple_of(me * rows, rows), rows)
        if c == 0:
            return [pltpu.make_async_copy(wk_hbm, w.at[0, at, pl.ds(0, HEAD)], load_sem.at[0]),
                    pltpu.make_async_copy(wv_hbm, w.at[0, at, pl.ds(HEAD, HEAD)], load_sem.at[chunks])]
        return [pltpu.make_async_copy(wq_hbm.at[:, pl.ds((c - 1) * PAIR, PAIR)], w.at[c, at], load_sem.at[c])]

    for c in range(chunks):
        for copy in loads(c):
            copy.start()

    def tok_copy(name):
        pos = BY_NAME[name]
        start = pl.multiple_of((lax.rem(zh + pos[0], 2) * 4 + lax.rem(x + pos[1], 4)) * 2 * rows, 1024)
        at = pl.ds(start, 2 * rows)
        return pltpu.make_async_copy(tok_hbm.at[:, at], tok.at[:, at], tok_sem.at[ALL.index(pos)])

    barrier = pltpu.get_barrier_semaphore()
    for target in (to_left, to_right, partner, sibling):
        pl.semaphore_signal(barrier, inc=1, device_id=target, device_id_type=MESH)
    pl.semaphore_wait(barrier, 4)

    head_count = 0
    while ORDER[head_count][0] == "own":
        for copy in loads(ORDER[head_count][1]):
            copy.wait()
        send_own(ORDER[head_count][1])
        head_count += 1
    for c in range(head_count, chunks):
        for copy in loads(c):
            copy.wait()

    for name in BY_NAME:
        tok_copy(name).start()

    for i in range(tokens // HEAD):
        mine = jnp.transpose(jnp.broadcast_to(seg_ref[i:i + 1, :], (HEAD, HEAD)))
        for j in range((i * HEAD // TILE + 1) * TILE // HEAD):
            ok = mine == jnp.broadcast_to(seg_ref[j:j + 1, :], (HEAD, HEAD))
            t = lax.broadcasted_iota(jnp.int32, (HEAD, HEAD), 0) + i * HEAD
            u = lax.broadcasted_iota(jnp.int32, (HEAD, HEAD), 1) + j * HEAD
            bias[i * HEAD:(i + 1) * HEAD, j * HEAD:(j + 1) * HEAD] = jnp.where(
                jnp.logical_and(ok, u <= t), jnp.float32(0.0), jnp.float32(NEGATIVE))

    steps = dict(own=send_own, x=take_x, z=take_z, far=send_far, halves=take_halves, take_far=take_far, corner=take_corner,
                 mul=project, round=round_chunk, attend=attend)
    seen = set()
    for step in ORDER[head_count:]:
        if step[0] == "mul" and step[2] not in seen:
            tok_copy(step[2]).wait()
            seen.add(step[2])
        steps[step[0]](*step[1:])

    def drain(c, carry):
        for slot, (pos, first, count) in enumerate(
                ((OWN, 0, rows), (OWN, 0, rows), (XP, 0, half), (XM, half, half), (ZO, 0, ROWS_X), (ZO, 0, ROWS_X),
                 (OWN, 0, rows), (X2, 0, rows), (XP, ROWS_X, rows - ROWS_X), (XM, ROWS_X, rows - ROWS_X))
                + tuple((pos, 0, rows) for pos in ALL)):
            if count > 0:
                ref = part(c, pos, 0, first, count)
                pltpu.make_async_remote_copy(
                    src_ref=ref, dst_ref=ref, send_sem=send_sem.at[c, slot], recv_sem=recv_sem.at[c, slot],
                    device_id=sibling, device_id_type=MESH).wait_send()
        return carry

    lax.fori_loop(0, chunks, drain, 0)

    def drain_out(c, carry):
        for h in range(2):
            out_copy(c, h).wait()
        return carry

    lax.fori_loop(1, chunks, drain_out, 0)


def body(tokens, w_query, key_weight, value_weight, segment_ids):
    seq, width = tokens.shape
    rows, columns = w_query.shape
    chunks = columns // PAIR + 1
    heads = columns // HEAD
    any_space = pl.BlockSpec(memory_space=pl.ANY)
    flops = 2 * seq * width * (columns + PAIR)
    return pl.pallas_call(
        kernel,
        out_shape=jax.ShapeDtypeStruct((seq, columns), jnp.bfloat16),
        in_specs=[any_space] * 4 + [pl.BlockSpec(memory_space=pltpu.VMEM)],
        out_specs=any_space,
        scratch_shapes=[
            pltpu.VMEM((seq, width), jnp.bfloat16),
            pltpu.VMEM((chunks, width, PAIR), jnp.bfloat16),
            pltpu.VMEM((seq, PAIR), jnp.float32),
            pltpu.VMEM((chunks, 2, seq, HEAD), jnp.bfloat16),
            pltpu.VMEM((seq, seq), jnp.float32),
            pltpu.VMEM((heads, seq, HEAD), jnp.bfloat16),
            pltpu.SemaphoreType.DMA((chunks + 1,)),
            pltpu.SemaphoreType.DMA((8,)),
            pltpu.SemaphoreType.DMA((heads,)),
            pltpu.SemaphoreType.DMA((chunks, LANE + BLOCKS)),
            pltpu.SemaphoreType.DMA((chunks, LANE + BLOCKS)),
        ],
        compiler_params=pltpu.CompilerParams(
            collective_id=0, has_side_effects=True, vmem_limit_bytes=58 * 2**20),
        cost_estimate=pl.CostEstimate(flops=flops, bytes_accessed=40 * 2**20, transcendentals=8 * seq * seq),
    )(tokens, w_query, key_weight, value_weight, segment_ids.reshape(seq // HEAD, HEAD))


def solution(mesh):
    in_specs = (P("dp", None), P("dp", "head"), P("dp", "head"), P("dp", "head"), P("dp"))
    return jax.shard_map(body, mesh=mesh, in_specs=in_specs, out_specs=P("dp", "head"), check_vma=False)
```

```python
import functools
import math

import jax
import jax.numpy as jnp
from jax import lax
from jax.experimental import pallas as pl
from jax.experimental.pallas import tpu as pltpu
from jax.sharding import PartitionSpec as P

MESH = pl.DeviceIdType.MESH
HEAD = 128
NEGATIVE = -1e30
EXP2_SCALE = math.log2(math.e) / math.sqrt(HEAD)
LANE = 14
BLOCKS = 8
ROWS_X = (416, 416, 416, 416, 416)
PIECES = (1, 1, 1, 1, 1)
MUL_RUN = 2
TILE_RUN = 4
TILE = 256

CHUNKS = ((0, 2), (2, 2), (4, 2), (6, 2), (8, 2))

ORDER = (
    ("own", 0), ("own", 1), ("own", 2), ("mul", 0, "OWN"), ("mul", 1, "OWN"), ("own", 3), ("x", 0), ("z", 0),
    ("mul", 0, "XP"), ("mul", 0, "XM"), ("mul", 0, "ZO"), ("x", 1), ("z", 1), ("mul", 1, "XP"),
    ("mul", 1, "XM"), ("mul", 1, "ZO"), ("x", 2), ("z", 2), ("x", 3), ("z", 3), ("halves", 0),
    ("mul", 0, "X2"), ("far", 0), ("halves", 1), ("mul", 1, "X2"), ("far", 1), ("halves", 2), ("far", 2),
    ("halves", 3), ("corner", 0), ("own", 4), ("take_far", 0), ("mul", 0, "CO"), ("mul", 0, "PP"),
    ("mul", 0, "PM"), ("far", 3), ("corner", 1), ("round", 0), ("mul", 2, "OWN"), ("take_far", 1),
    ("mul", 2, "XP"), ("mul", 2, "XM"), ("mul", 1, "CO"), ("mul", 2, "ZO"), ("mul", 2, "X2"), ("mul", 1, "PP"),
    ("mul", 1, "PM"), ("take_far", 2), ("round", 1), ("corner", 2), ("attend", 1, 0), ("attend", 1, 1),
    ("attend", 1, 2), ("attend", 1, 3), ("mul", 2, "PP"), ("mul", 2, "CO"), ("mul", 2, "PM"), ("round", 2),
    ("attend", 2, 0), ("attend", 2, 1), ("x", 4), ("corner", 3), ("attend", 2, 2), ("attend", 2, 3),
    ("mul", 3, "OWN"), ("mul", 3, "XP"), ("mul", 3, "XM"), ("mul", 3, "ZO"), ("take_far", 3), ("mul", 3, "X2"),
    ("mul", 3, "CO"), ("z", 4), ("far", 4), ("mul", 4, "OWN"), ("mul", 4, "XP"), ("halves", 4),
    ("mul", 3, "PP"), ("mul", 3, "PM"), ("round", 3), ("attend", 3, 0), ("attend", 3, 1), ("attend", 3, 2),
    ("attend", 3, 3), ("mul", 4, "XM"), ("take_far", 4), ("mul", 4, "ZO"), ("mul", 4, "X2"), ("corner", 4),
    ("mul", 4, "PP"), ("mul", 4, "PM"), ("mul", 4, "CO"), ("round", 4), ("attend", 4, 0), ("attend", 4, 1),
    ("attend", 4, 2), ("attend", 4, 3),
)


def kernel(tok_hbm, wq_hbm, wk_hbm, wv_hbm, seg_ref, out, tok, acc, qkv, bias,
           load_sem, tok_sem, send_sem, recv_sem, *w):
    tokens = tok.shape[0]
    rows = wq_hbm.shape[0]
    half = rows // 2
    me = lax.axis_index("dp")
    head = lax.axis_index("head")
    zh, x, core = me // 8, lax.rem(me // 2, 4), lax.rem(me, 2)

    def device(dz, dx, dc):
        return (lax.rem(zh + dz, 2) * 4 + lax.rem(x + dx, 4)) * 2 + lax.rem(core + dc, 2)

    OWN, XP, XM, X2, ZO, PP, PM, CO = (0, 0), (0, 1), (0, 3), (0, 2), (1, 0), (1, 1), (1, 3), (1, 2)
    ALL = (OWN, XP, XM, X2, ZO, PP, PM, CO)
    BY_NAME = dict(OWN=OWN, XP=XP, XM=XM, X2=X2, ZO=ZO, PP=PP, PM=PM, CO=CO)
    to_left, to_right = (device(0, 3, 0), head), (device(0, 1, 0), head)
    partner, sibling = (device(1, 0, 0), head), (device(0, 0, 1), head)

    def apart(work):
        pl.when(me >= 0)(work)

    def part(c, pos, dc, first, count):
        start = pl.multiple_of(device(pos[0], pos[1], dc) * rows + first, 16)
        return w[c].at[pl.ds(start, count)]

    def send(c, pos, first, count, target, slot):
        ref = part(c, pos, 0, first, count)
        pltpu.make_async_remote_copy(
            src_ref=ref, dst_ref=ref, send_sem=send_sem.at[c, slot], recv_sem=recv_sem.at[c, slot],
            device_id=target, device_id_type=MESH).start()

    def pair(c, pos):
        send(c, pos, 0, rows, sibling, LANE + ALL.index(pos))

    def wait(c, pos, first, count, slot, dc=0):
        ref = part(c, pos, dc, first, count)
        pltpu.make_async_remote_copy(
            src_ref=ref, dst_ref=ref, send_sem=send_sem.at[c, slot], recv_sem=recv_sem.at[c, slot],
            device_id=sibling, device_id_type=MESH).wait_recv()

    def send_own(c):
        send(c, OWN, 0, rows, to_left, 0)
        send(c, OWN, 0, rows, to_right, 1)
        send(c, OWN, 0, rows, partner, 6)
        pair(c, OWN)

    def take_x(c):
        wait(c, XP, 0, rows, 0)
        send(c, XP, 0, half, to_left, 2)
        wait(c, XM, 0, rows, 1)
        send(c, XM, half, half, to_right, 3)
        if ROWS_X[c] < rows:
            send(c, XP, ROWS_X[c], rows - ROWS_X[c], partner, 8)
            send(c, XM, ROWS_X[c], rows - ROWS_X[c], partner, 9)
        pair(c, XP)
        pair(c, XM)

    def take_z(c):
        wait(c, ZO, 0, rows, 6)
        pair(c, ZO)

    def pieces(c):
        size = ROWS_X[c] // PIECES[c]
        return [(i * size, size) for i in range(PIECES[c])]

    def send_far(c):
        for i, (first, count) in enumerate(pieces(c)):
            send(c, ZO, first, count, to_left, (4, 10)[i])
            send(c, ZO, first, count, to_right, (5, 11)[i])

    def take_halves(c):
        wait(c, X2, 0, half, 2)
        wait(c, X2, half, half, 3)
        send(c, X2, 0, rows, partner, 7)
        pair(c, X2)

    def take_far(c):
        if ROWS_X[c] < rows:
            wait(c, PP, ROWS_X[c], rows - ROWS_X[c], 8)
            wait(c, PM, ROWS_X[c], rows - ROWS_X[c], 9)
        for i, (first, count) in enumerate(pieces(c)):
            on = rows - first if i == PIECES[c] - 1 else count
            wait(c, PP, first, count, (4, 10)[i])
            send(c, PP, first, on, sibling, (LANE + 5, 12)[i])
            wait(c, PM, first, count, (5, 11)[i])
            send(c, PM, first, on, sibling, (LANE + 6, 13)[i])

    def sibling_pieces(c, pos):
        slot = LANE + ALL.index(pos)
        if pos not in (PP, PM) or PIECES[c] == 1:
            return [(0, rows, slot)]
        size = ROWS_X[c] // PIECES[c]
        return [(0, size, slot), (size, rows - size, 12 if pos == PP else 13)]

    def take_corner(c):
        wait(c, CO, 0, rows, 7)
        pair(c, CO)

    started = set()

    def first_column(pos):
        return pl.multiple_of((lax.rem(zh + pos[0], 2) * 4 + lax.rem(x + pos[1], 4)) * 2 * rows, 1024)

    def project(c, names):
        positions = [BY_NAME[name] for name in names]
        for pos in positions:
            for first, count, slot in sibling_pieces(c, pos):
                wait(c, pos, first, count, slot, dc=1)
        columns = slice(0, w[c].shape[1])
        fresh = c not in started
        started.add(c)

        def multiply():
            total = None if fresh else acc[c % 2, :, columns]
            for pos in positions:
                at = pl.ds(first_column(pos), 2 * rows)
                part_sum = jnp.dot(tok[:, at], w[c][at], preferred_element_type=jnp.float32)
                total = part_sum if total is None else total + part_sum
            acc[c % 2, :, columns] = total

        apart(multiply)

    def round_chunk(c):
        def rounded():
            for h in range(CHUNKS[c][1]):
                qkv[CHUNKS[c][0] + h] = acc[c % 2, :, h * HEAD:(h + 1) * HEAD].astype(jnp.bfloat16)

        apart(rounded)

    def attend(c, ids):
        first, count = CHUNKS[c]
        tiles = tokens // TILE

        def tile_pair(i):
            work = [(first + h, i) for h in range(2)] if count == 2 else [(first, i), (first, tiles - 1 - i)]
            scores = [lax.dot_general(qkv[h, j * TILE:(j + 1) * TILE], qkv[0, :(j + 1) * TILE], (((1,), (1,)), ((), ())),
                                      preferred_element_type=jnp.float32)
                      + bias[j * TILE:(j + 1) * TILE, :(j + 1) * TILE] for h, j in work]
            weights = [jnp.exp2((s - jnp.max(s, axis=1, keepdims=True)) * EXP2_SCALE) for s in scores]
            for (h, j), p in zip(work, weights):
                total = jnp.sum(p, axis=1, keepdims=True)
                o = jnp.dot(p.astype(jnp.bfloat16), qkv[1, :(j + 1) * TILE], preferred_element_type=jnp.float32)
                out[j * TILE:(j + 1) * TILE, (h - 2) * HEAD:(h - 1) * HEAD] = (o / total).astype(jnp.bfloat16)

        def all_pairs():
            for i in ids:
                tile_pair(i)

        apart(all_pairs)

    def loads(c):
        at = pl.ds(pl.multiple_of(me * rows, rows), rows)
        if c == 0:
            return [pltpu.make_async_copy(wk_hbm, w[0].at[at, pl.ds(0, HEAD)], load_sem.at[0]),
                    pltpu.make_async_copy(wv_hbm, w[0].at[at, pl.ds(HEAD, HEAD)], load_sem.at[len(CHUNKS)])]
        first, count = CHUNKS[c]
        return [pltpu.make_async_copy(
            wq_hbm.at[:, pl.ds((first - 2) * HEAD, count * HEAD)], w[c].at[at], load_sem.at[c])]

    def tok_copy(name):
        at = pl.ds(first_column(BY_NAME[name]), 2 * rows)
        return pltpu.make_async_copy(tok_hbm.at[:, at], tok.at[:, at], tok_sem.at[ALL.index(BY_NAME[name])])

    for c in range(len(CHUNKS)):
        for copy in loads(c):
            copy.start()

    barrier = pltpu.get_barrier_semaphore()
    for target in (to_left, to_right, partner, sibling):
        pl.semaphore_signal(barrier, inc=1, device_id=target, device_id_type=MESH)
    pl.semaphore_wait(barrier, 4)

    begun = 0
    while ORDER[begun][0] == "own":
        for copy in loads(ORDER[begun][1]):
            copy.wait()
        send_own(ORDER[begun][1])
        begun += 1
    for c in range(begun, len(CHUNKS)):
        for copy in loads(c):
            copy.wait()
    for name in BY_NAME:
        tok_copy(name).start()

    def fill_mask():
        for i in range(tokens // HEAD):
            mine = jnp.transpose(jnp.broadcast_to(seg_ref[i:i + 1, :], (HEAD, HEAD)))
            for j in range((i * HEAD // TILE + 1) * TILE // HEAD):
                ok = mine == jnp.broadcast_to(seg_ref[j:j + 1, :], (HEAD, HEAD))
                t = lax.broadcasted_iota(jnp.int32, (HEAD, HEAD), 0) + i * HEAD
                u = lax.broadcasted_iota(jnp.int32, (HEAD, HEAD), 1) + j * HEAD
                bias[i * HEAD:(i + 1) * HEAD, j * HEAD:(j + 1) * HEAD] = jnp.where(
                    jnp.logical_and(ok, u <= t), jnp.float32(0.0), jnp.float32(NEGATIVE))

    apart(fill_mask)

    steps = dict(own=send_own, x=take_x, z=take_z, far=send_far, halves=take_halves, take_far=take_far, corner=take_corner,
                 mul=project, round=round_chunk, attend=attend)
    runs = []
    for step in ORDER[begun:]:
        if len(step) == 2:
            runs.append(step)
        elif runs and runs[-1][:2] == step[:2] and (
                len(runs[-1][2]) < MUL_RUN if step[0] == "mul" else sum(i + 1 for i in runs[-1][2]) + step[2] < TILE_RUN):
            runs[-1][2].append(step[2])
        else:
            runs.append((step[0], step[1], [step[2]]))
    seen = set()
    for run in runs:
        if run[0] == "mul":
            for name in run[2]:
                if name not in seen:
                    tok_copy(name).wait()
                    seen.add(name)
        steps[run[0]](*run[1:])

    for c in range(len(CHUNKS)):
        far = pieces(c) + [(0, 0)]
        rest = rows - ROWS_X[c]
        on = [sibling_pieces(c, pos) for pos in ALL]
        for slot, (pos, first, count) in enumerate(
                [(OWN, 0, rows), (OWN, 0, rows), (XP, 0, half), (XM, half, half), (ZO,) + far[0], (ZO,) + far[0],
                 (OWN, 0, rows), (X2, 0, rows), (XP, ROWS_X[c], rest), (XM, ROWS_X[c], rest), (ZO,) + far[1], (ZO,) + far[1]]
                + [(pos,) + (on[ALL.index(pos)] + [(0, 0)])[1][:2] for pos in (PP, PM)]
                + [(pos,) + on[i][0][:2] for i, pos in enumerate(ALL)]):
            if count > 0:
                ref = part(c, pos, 0, first, count)
                pltpu.make_async_remote_copy(
                    src_ref=ref, dst_ref=ref, send_sem=send_sem.at[c, slot], recv_sem=recv_sem.at[c, slot],
                    device_id=sibling, device_id_type=MESH).wait_send()


def body(tokens, w_query, key_weight, value_weight, segment_ids):
    seq, width = tokens.shape
    columns = w_query.shape[1]
    heads = columns // HEAD
    any_space = pl.BlockSpec(memory_space=pl.ANY)
    in_vmem = pl.BlockSpec(memory_space=pltpu.VMEM)
    return pl.pallas_call(
        kernel,
        out_shape=pltpu.VMEM((seq, columns), jnp.bfloat16),
        in_specs=[any_space] * 4 + [in_vmem],
        out_specs=in_vmem,
        scratch_shapes=[
            pltpu.VMEM((seq, width), jnp.bfloat16),
            pltpu.VMEM((2, seq, 2 * HEAD), jnp.float32),
            pltpu.VMEM((heads + 2, seq, HEAD), jnp.bfloat16),
            pltpu.VMEM((seq, seq), jnp.float32),
            pltpu.SemaphoreType.DMA((len(CHUNKS) + 1,)),
            pltpu.SemaphoreType.DMA((8,)),
            pltpu.SemaphoreType.DMA((len(CHUNKS), LANE + BLOCKS)),
            pltpu.SemaphoreType.DMA((len(CHUNKS), LANE + BLOCKS)),
        ] + [pltpu.VMEM((width, count * HEAD), jnp.bfloat16) for _, count in CHUNKS],
        compiler_params=pltpu.CompilerParams(
            collective_id=0, has_side_effects=True, vmem_limit_bytes=58 * 2**20),
        cost_estimate=pl.CostEstimate(
            flops=2 * seq * width * (columns + 2 * HEAD), bytes_accessed=40 * 2**20, transcendentals=heads * seq * seq),
    )(tokens, w_query, key_weight, value_weight, segment_ids.reshape(seq // HEAD, HEAD))


def solution(mesh):
    in_specs = (P("dp", None), P("dp", "head"), P("dp", "head"), P("dp", "head"), P("dp"))
    return jax.shard_map(body, mesh=mesh, in_specs=in_specs, out_specs=P("dp", "head"), check_vma=False)
```

```python
import functools
import math

import jax
import jax.numpy as jnp
from jax import lax
from jax.experimental import pallas as pl
from jax.experimental.pallas import tpu as pltpu
from jax.sharding import PartitionSpec as P

MESH = pl.DeviceIdType.MESH
HEAD = 128
NEGATIVE = -1e30
EXP2_SCALE = math.log2(math.e) / math.sqrt(HEAD)
LANE = 14
BLOCKS = 8
ROWS_X = (400, 384, 448, 368, 480)
PIECES = (1, 1, 1, 1, 1)
MUL_RUN = 2
TILE_RUN = 4
TILE = 256

CHUNKS = ((0, 2), (2, 2), (4, 2), (6, 2), (8, 2))

ORDER = (
    ("own", 0), ("own", 1), ("z", 0), ("x", 0), ("mul", 0, "XM"), ("own", 2), ("x", 1), ("halves", 0),
    ("z", 1), ("mul", 0, "X2"), ("far", 1), ("far", 0), ("mul", 0, "XP"), ("halves", 1), ("x", 2), ("own", 3),
    ("z", 2), ("corner", 0), ("take_far", 1), ("take_far", 0), ("mul", 0, "CO"), ("mul", 0, "OWN"),
    ("mul", 1, "ZO"), ("mul", 1, "PP"), ("mul", 1, "X2"), ("mul", 0, "PM"), ("corner", 1), ("mul", 1, "XM"),
    ("far", 2), ("mul", 0, "ZO"), ("mul", 0, "PP"), ("halves", 2), ("round", 0), ("mul", 1, "XP"),
    ("mul", 2, "ZO"), ("mul", 2, "XM"), ("x", 3), ("mul", 1, "CO"), ("mul", 2, "XP"), ("mul", 1, "OWN"),
    ("mul", 2, "OWN"), ("mul", 1, "PM"), ("round", 1), ("take_far", 2), ("mul", 3, "XP"), ("attend", 1, 0),
    ("own", 4), ("attend", 1, 2), ("attend", 1, 3), ("z", 3), ("corner", 2), ("mul", 3, "XM"),
    ("mul", 2, "PM"), ("attend", 1, 1), ("far", 3), ("mul", 2, "X2"), ("halves", 3), ("mul", 3, "OWN"),
    ("mul", 2, "PP"), ("mul", 2, "CO"), ("round", 2), ("mul", 3, "ZO"), ("x", 4), ("attend", 2, 3), ("z", 4),
    ("attend", 2, 0), ("attend", 2, 2), ("far", 4), ("mul", 4, "XM"), ("take_far", 3), ("mul", 3, "X2"),
    ("mul", 4, "ZO"), ("attend", 2, 1), ("mul", 4, "XP"), ("halves", 4), ("mul", 4, "OWN"), ("corner", 3),
    ("mul", 3, "PM"), ("mul", 3, "PP"), ("mul", 4, "X2"), ("mul", 3, "CO"), ("round", 3), ("attend", 3, 0),
    ("attend", 3, 3), ("take_far", 4), ("attend", 3, 1), ("part", 4, "PM", 0), ("attend", 3, 2), ("corner", 4),
    ("part", 4, "CO", 0), ("part", 4, "PP", 0), ("part", 4, "PP", 1), ("part", 4, "PM", 1),
    ("part", 4, "CO", 1), ("round", 4), ("attend", 4, 3), ("attend", 4, 0), ("attend", 4, 2), ("attend", 4, 1),
)


def kernel(tok_hbm, wq_hbm, wk_hbm, wv_hbm, seg_hbm, out, tok, acc, qkv, bias, seg_ref,
           load_sem, tok_sem, seg_sem, send_sem, recv_sem, *w):
    tokens = tok.shape[0]
    rows = wq_hbm.shape[0]
    half = rows // 2
    last = len(CHUNKS) - 1
    me = lax.axis_index("dp")
    head = lax.axis_index("head")
    zh, x, core = me // 8, lax.rem(me // 2, 4), lax.rem(me, 2)

    def device(dz, dx, dc):
        return (lax.rem(zh + dz, 2) * 4 + lax.rem(x + dx, 4)) * 2 + lax.rem(core + dc, 2)

    OWN, XP, XM, X2, ZO, PP, PM, CO = (0, 0), (0, 1), (0, 3), (0, 2), (1, 0), (1, 1), (1, 3), (1, 2)
    ALL = (OWN, XP, XM, X2, ZO, PP, PM, CO)
    BY_NAME = dict(OWN=OWN, XP=XP, XM=XM, X2=X2, ZO=ZO, PP=PP, PM=PM, CO=CO)
    to_left, to_right = (device(0, 3, 0), head), (device(0, 1, 0), head)
    partner, sibling = (device(1, 0, 0), head), (device(0, 0, 1), head)

    def apart(work):
        pl.when(me >= 0)(work)

    def part(c, pos, dc, first, count):
        start = pl.multiple_of(device(pos[0], pos[1], dc) * rows + first, 16)
        return w[c].at[pl.ds(start, count)]

    def send(c, pos, first, count, target, slot):
        ref = part(c, pos, 0, first, count)
        pltpu.make_async_remote_copy(
            src_ref=ref, dst_ref=ref, send_sem=send_sem.at[c, slot], recv_sem=recv_sem.at[c, slot],
            device_id=target, device_id_type=MESH).start()

    def pair(c, pos):
        send(c, pos, 0, rows, sibling, LANE + ALL.index(pos))

    def wait(c, pos, first, count, slot, dc=0):
        ref = part(c, pos, dc, first, count)
        pltpu.make_async_remote_copy(
            src_ref=ref, dst_ref=ref, send_sem=send_sem.at[c, slot], recv_sem=recv_sem.at[c, slot],
            device_id=sibling, device_id_type=MESH).wait_recv()

    def send_own(c):
        send(c, OWN, 0, rows, to_left, 0)
        send(c, OWN, 0, rows, to_right, 1)
        send(c, OWN, 0, rows, partner, 6)
        pair(c, OWN)

    def take_x(c):
        wait(c, XP, 0, rows, 0)
        send(c, XP, 0, half, to_left, 2)
        wait(c, XM, 0, rows, 1)
        send(c, XM, half, half, to_right, 3)
        if ROWS_X[c] < rows:
            send(c, XP, ROWS_X[c], rows - ROWS_X[c], partner, 8)
            send(c, XM, ROWS_X[c], rows - ROWS_X[c], partner, 9)
        pair(c, XP)
        pair(c, XM)

    def take_z(c):
        wait(c, ZO, 0, rows, 6)
        pair(c, ZO)

    def pieces(c):
        size = ROWS_X[c] // PIECES[c]
        return [(i * size, size) for i in range(PIECES[c])]

    def send_far(c):
        for i, (first, count) in enumerate(pieces(c)):
            send(c, ZO, first, count, to_left, (4, 10)[i])
            send(c, ZO, first, count, to_right, (5, 11)[i])

    def take_halves(c):
        wait(c, X2, 0, half, 2)
        wait(c, X2, half, half, 3)
        send(c, X2, 0, rows, partner, 7)
        pair(c, X2)

    def take_far(c):
        if ROWS_X[c] < rows:
            wait(c, PP, ROWS_X[c], rows - ROWS_X[c], 8)
            wait(c, PM, ROWS_X[c], rows - ROWS_X[c], 9)
        for i, (first, count) in enumerate(pieces(c)):
            on = rows - first if i == PIECES[c] - 1 else count
            wait(c, PP, first, count, (4, 10)[i])
            send(c, PP, first, on, sibling, (LANE + 5, 12)[i])
            wait(c, PM, first, count, (5, 11)[i])
            send(c, PM, first, on, sibling, (LANE + 6, 13)[i])

    def sibling_pieces(c, pos):
        slot = LANE + ALL.index(pos)
        if pos not in (PP, PM) or PIECES[c] == 1:
            return [(0, rows, slot)]
        size = ROWS_X[c] // PIECES[c]
        return [(0, size, slot), (size, rows - size, 12 if pos == PP else 13)]

    def take_corner(c):
        wait(c, CO, 0, rows, 7)
        pair(c, CO)

    started = set()

    def first_column(pos):
        return pl.multiple_of((lax.rem(zh + pos[0], 2) * 4 + lax.rem(x + pos[1], 4)) * 2 * rows, 1024)

    def project(c, names):
        positions = [BY_NAME[name] for name in names]
        for pos in positions:
            for first, count, slot in sibling_pieces(c, pos):
                wait(c, pos, first, count, slot, dc=1)
        columns = slice(0, w[c].shape[1])
        fresh = c not in started
        started.add(c)

        def multiply():
            total = None if fresh else acc[c % 2, :, columns]
            for pos in positions:
                at = pl.ds(first_column(pos), 2 * rows)
                part_sum = jnp.dot(tok[:, at], w[c][at], preferred_element_type=jnp.float32)
                total = part_sum if total is None else total + part_sum
            acc[c % 2, :, columns] = total

        apart(multiply)

    def project_part(c, name, dc):
        pos = BY_NAME[name]
        if dc == 1:
            for first, count, slot in sibling_pieces(c, pos):
                wait(c, pos, first, count, slot, dc=1)
        columns = slice(0, w[c].shape[1])
        at = pl.ds(pl.multiple_of(device(pos[0], pos[1], dc) * rows, 512), rows)

        def multiply():
            acc[c % 2, :, columns] += jnp.dot(tok[:, at], w[c][at], preferred_element_type=jnp.float32)

        apart(multiply)

    def round_chunk(c):
        def rounded():
            for h in range(CHUNKS[c][1]):
                qkv[CHUNKS[c][0] + h] = acc[c % 2, :, h * HEAD:(h + 1) * HEAD].astype(jnp.bfloat16)

        apart(rounded)

    def attend(c, ids):
        first, count = CHUNKS[c]
        tiles = tokens // TILE

        def tile_pair(i):
            work = [(first + h, i) for h in range(2)] if count == 2 else [(first, i), (first, tiles - 1 - i)]
            scores = [lax.dot_general(qkv[h, j * TILE:(j + 1) * TILE], qkv[0, :(j + 1) * TILE], (((1,), (1,)), ((), ())),
                                      preferred_element_type=jnp.float32)
                      + bias[j * TILE:(j + 1) * TILE, :(j + 1) * TILE] for h, j in work]
            weights = [jnp.exp2((s - jnp.max(s, axis=1, keepdims=True)) * EXP2_SCALE) for s in scores]
            for (h, j), p in zip(work, weights):
                total = jnp.sum(p, axis=1, keepdims=True)
                o = jnp.dot(p.astype(jnp.bfloat16), qkv[1, :(j + 1) * TILE], preferred_element_type=jnp.float32)
                out[j * TILE:(j + 1) * TILE, (h - 2) * HEAD:(h - 1) * HEAD] = (o / total).astype(jnp.bfloat16)

        def all_pairs():
            for i in ids:
                tile_pair(i)

        apart(all_pairs)

    def loads(c):
        at = pl.ds(pl.multiple_of(me * rows, rows), rows)
        if c == 0:
            return [pltpu.make_async_copy(wk_hbm, w[0].at[at, pl.ds(0, HEAD)], load_sem.at[0]),
                    pltpu.make_async_copy(wv_hbm, w[0].at[at, pl.ds(HEAD, HEAD)], load_sem.at[len(CHUNKS)])]
        first, count = CHUNKS[c]
        return [pltpu.make_async_copy(
            wq_hbm.at[:, pl.ds((first - 2) * HEAD, count * HEAD)], w[c].at[at], load_sem.at[c])]

    def tok_copy(name):
        at = pl.ds(first_column(BY_NAME[name]), 2 * rows)
        return pltpu.make_async_copy(tok_hbm.at[:, at], tok.at[:, at], tok_sem.at[ALL.index(BY_NAME[name])])

    for c in range(len(CHUNKS)):
        for copy in loads(c):
            copy.start()

    barrier = pltpu.get_barrier_semaphore()
    for target in (to_left, to_right, partner, sibling):
        pl.semaphore_signal(barrier, inc=1, device_id=target, device_id_type=MESH)
    pl.semaphore_wait(barrier, 4)

    begun = 0
    while ORDER[begun][0] == "own":
        for copy in loads(ORDER[begun][1]):
            copy.wait()
        send_own(ORDER[begun][1])
        begun += 1
    for c in range(begun, len(CHUNKS)):
        for copy in loads(c):
            copy.wait()
    seg_copy = pltpu.make_async_copy(seg_hbm, seg_ref, seg_sem)
    seg_copy.start()
    for name in BY_NAME:
        tok_copy(name).start()
    seg_copy.wait()

    def fill_mask():
        for i in range(tokens // HEAD):
            mine = jnp.transpose(jnp.broadcast_to(seg_ref[i:i + 1, :], (HEAD, HEAD)))
            for j in range((i * HEAD // TILE + 1) * TILE // HEAD):
                ok = mine == jnp.broadcast_to(seg_ref[j:j + 1, :], (HEAD, HEAD))
                t = lax.broadcasted_iota(jnp.int32, (HEAD, HEAD), 0) + i * HEAD
                u = lax.broadcasted_iota(jnp.int32, (HEAD, HEAD), 1) + j * HEAD
                bias[i * HEAD:(i + 1) * HEAD, j * HEAD:(j + 1) * HEAD] = jnp.where(
                    jnp.logical_and(ok, u <= t), jnp.float32(0.0), jnp.float32(NEGATIVE))

    apart(fill_mask)

    def drain(c):
        far = pieces(c) + [(0, 0)]
        rest = rows - ROWS_X[c]
        on = [sibling_pieces(c, pos) for pos in ALL]
        for slot, (pos, first, count) in enumerate(
                [(OWN, 0, rows), (OWN, 0, rows), (XP, 0, half), (XM, half, half), (ZO,) + far[0], (ZO,) + far[0],
                 (OWN, 0, rows), (X2, 0, rows), (XP, ROWS_X[c], rest), (XM, ROWS_X[c], rest), (ZO,) + far[1], (ZO,) + far[1]]
                + [(pos,) + (on[ALL.index(pos)] + [(0, 0)])[1][:2] for pos in (PP, PM)]
                + [(pos,) + on[i][0][:2] for i, pos in enumerate(ALL)]):
            if count > 0:
                ref = part(c, pos, 0, first, count)
                pltpu.make_async_remote_copy(
                    src_ref=ref, dst_ref=ref, send_sem=send_sem.at[c, slot], recv_sem=recv_sem.at[c, slot],
                    device_id=sibling, device_id_type=MESH).wait_send()

    steps = dict(own=send_own, x=take_x, z=take_z, far=send_far, halves=take_halves, take_far=take_far, corner=take_corner,
                 mul=project, part=project_part, round=round_chunk, attend=attend)
    runs = []
    for step in ORDER[begun:]:
        if len(step) != 3:
            runs.append(step)
        elif runs and runs[-1][:2] == step[:2] and (
                len(runs[-1][2]) < MUL_RUN if step[0] == "mul" else sum(i + 1 for i in runs[-1][2]) + step[2] < TILE_RUN):
            runs[-1][2].append(step[2])
        else:
            runs.append((step[0], step[1], [step[2]]))
    seen = set()
    drained = False
    for run in runs:
        if run[1] == last and run[0] in ("take_far", "corner") and not drained:
            for c in range(last):
                drain(c)
            drained = True
        if run[0] == "mul":
            for name in run[2]:
                if name not in seen:
                    tok_copy(name).wait()
                    seen.add(name)
        steps[run[0]](*run[1:])

    drain(last)


def body(tokens, w_query, key_weight, value_weight, segment_ids):
    seq, width = tokens.shape
    columns = w_query.shape[1]
    heads = columns // HEAD
    any_space = pl.BlockSpec(memory_space=pl.ANY)
    in_vmem = pl.BlockSpec(memory_space=pltpu.VMEM)
    return pl.pallas_call(
        kernel,
        out_shape=pltpu.VMEM((seq, columns), jnp.bfloat16),
        in_specs=[any_space] * 5,
        out_specs=in_vmem,
        scratch_shapes=[
            pltpu.VMEM((seq, width), jnp.bfloat16),
            pltpu.VMEM((2, seq, 2 * HEAD), jnp.float32),
            pltpu.VMEM((heads + 2, seq, HEAD), jnp.bfloat16),
            pltpu.VMEM((seq, seq), jnp.float32),
            pltpu.VMEM((seq // HEAD, HEAD), jnp.int32),
            pltpu.SemaphoreType.DMA((len(CHUNKS) + 1,)),
            pltpu.SemaphoreType.DMA((8,)),
            pltpu.SemaphoreType.DMA,
            pltpu.SemaphoreType.DMA((len(CHUNKS), LANE + BLOCKS)),
            pltpu.SemaphoreType.DMA((len(CHUNKS), LANE + BLOCKS)),
        ] + [pltpu.VMEM((width, count * HEAD), jnp.bfloat16) for _, count in CHUNKS],
        compiler_params=pltpu.CompilerParams(
            collective_id=0, has_side_effects=True, vmem_limit_bytes=58 * 2**20),
        cost_estimate=pl.CostEstimate(
            flops=2 * seq * width * (columns + 2 * HEAD), bytes_accessed=40 * 2**20, transcendentals=heads * seq * seq),
    )(tokens, w_query, key_weight, value_weight, segment_ids.reshape(seq // HEAD, HEAD))


def solution(mesh):
    in_specs = (P("dp", None), P("dp", "head"), P("dp", "head"), P("dp", "head"), P("dp"))
    return jax.shard_map(body, mesh=mesh, in_specs=in_specs, out_specs=P("dp", "head"), check_vma=False)
```

```python
import functools
import math

import jax
import jax.numpy as jnp
from jax import lax
from jax.experimental import pallas as pl
from jax.experimental.pallas import tpu as pltpu
from jax.sharding import PartitionSpec as P

MESH = pl.DeviceIdType.MESH
HEAD = 128
NEGATIVE = -1e30
EXP2_SCALE = math.log2(math.e) / math.sqrt(HEAD)
LANE = 14
BLOCKS = 8
ROWS_X = (368, 400, 448, 384, 480)
PIECES = (1, 1, 1, 1, 1)
MUL_RUN = 2
TILE_RUN = 4
TILE = 256

CHUNKS = ((0, 2), (2, 2), (4, 2), (6, 2), (8, 2))

ORDER = (
    ("own", 0), ("own", 1), ("z", 0), ("x", 0), ("far", 0), ("own", 2), ("z", 1), ("take_far", 0),
    ("halves", 0), ("x", 1), ("x", 2), ("mul", 0, "XM"), ("corner", 0), ("z", 2), ("mul", 1, "ZO"),
    ("mul", 0, "PP"), ("halves", 1), ("far", 1), ("far", 2), ("mul", 1, "XP"), ("mul", 0, "XP"),
    ("mul", 0, "CO"), ("halves", 2), ("mul", 1, "XM"), ("mul", 0, "PM"), ("mul", 1, "OWN"), ("mul", 0, "OWN"),
    ("take_far", 1), ("mul", 0, "X2"), ("own", 3), ("mul", 0, "ZO"), ("round", 0), ("own", 4),
    ("mul", 2, "XP"), ("corner", 1), ("mul", 1, "X2"), ("mul", 2, "X2"), ("mul", 2, "XM"), ("take_far", 2),
    ("mul", 2, "OWN"), ("mul", 1, "PP"), ("mul", 1, "CO"), ("mul", 2, "PM"), ("mul", 1, "PM"), ("corner", 2),
    ("mul", 2, "PP"), ("round", 1), ("x", 3), ("mul", 2, "CO"), ("attend", 1, 2), ("mul", 2, "ZO"),
    ("attend", 1, 3), ("round", 2), ("attend", 1, 0), ("attend", 2, 3), ("attend", 1, 1), ("z", 3), ("far", 3),
    ("attend", 2, 1), ("attend", 2, 0), ("mul", 4, "OWN"), ("mul", 3, "OWN"), ("halves", 3), ("z", 4),
    ("x", 4), ("mul", 3, "XM"), ("far", 4), ("mul", 3, "ZO"), ("mul", 3, "XP"), ("attend", 2, 2),
    ("mul", 4, "ZO"), ("take_far", 3), ("mul", 3, "X2"), ("mul", 4, "XP"), ("mul", 4, "XM"), ("halves", 4),
    ("mul", 3, "PP"), ("corner", 3), ("mul", 3, "PM"), ("mul", 4, "X2"), ("mul", 3, "CO"), ("round", 3),
    ("attend", 3, 0), ("attend", 3, 1), ("attend", 3, 2), ("take_far", 4), ("attend", 3, 3),
    ("part", 4, "PP", 0), ("corner", 4), ("part", 4, "CO", 0), ("part", 4, "PM", 0), ("part", 4, "PP", 1),
    ("part", 4, "PM", 1), ("part", 4, "CO", 1), ("round", 4), ("attend", 4, 1), ("attend", 4, 3),
    ("attend", 4, 2), ("attend", 4, 0),
)


def kernel(tok_hbm, wq_hbm, wk_hbm, wv_hbm, seg_hbm, out, tok, acc, qkv, bias, seg_ref,
           load_sem, tok_sem, seg_sem, send_sem, recv_sem, *w):
    tokens = tok.shape[0]
    rows = wq_hbm.shape[0]
    half = rows // 2
    last = len(CHUNKS) - 1
    me = lax.axis_index("dp")
    head = lax.axis_index("head")
    zh, x, core = me // 8, lax.rem(me // 2, 4), lax.rem(me, 2)

    def device(dz, dx, dc):
        return (lax.rem(zh + dz, 2) * 4 + lax.rem(x + dx, 4)) * 2 + lax.rem(core + dc, 2)

    OWN, XP, XM, X2, ZO, PP, PM, CO = (0, 0), (0, 1), (0, 3), (0, 2), (1, 0), (1, 1), (1, 3), (1, 2)
    ALL = (OWN, XP, XM, X2, ZO, PP, PM, CO)
    BY_NAME = dict(OWN=OWN, XP=XP, XM=XM, X2=X2, ZO=ZO, PP=PP, PM=PM, CO=CO)
    to_left, to_right = (device(0, 3, 0), head), (device(0, 1, 0), head)
    partner, sibling = (device(1, 0, 0), head), (device(0, 0, 1), head)

    def apart(work):
        pl.when(me >= 0)(work)

    def part(c, pos, dc, first, count):
        start = pl.multiple_of(device(pos[0], pos[1], dc) * rows + first, 16)
        return w[c].at[pl.ds(start, count)]

    def send(c, pos, first, count, target, slot):
        ref = part(c, pos, 0, first, count)
        pltpu.make_async_remote_copy(
            src_ref=ref, dst_ref=ref, send_sem=send_sem.at[c, slot], recv_sem=recv_sem.at[c, slot],
            device_id=target, device_id_type=MESH).start()

    def pair(c, pos):
        send(c, pos, 0, rows, sibling, LANE + ALL.index(pos))

    def wait(c, pos, first, count, slot, dc=0):
        ref = part(c, pos, dc, first, count)
        pltpu.make_async_remote_copy(
            src_ref=ref, dst_ref=ref, send_sem=send_sem.at[c, slot], recv_sem=recv_sem.at[c, slot],
            device_id=sibling, device_id_type=MESH).wait_recv()

    def send_own(c):
        send(c, OWN, 0, rows, to_left, 0)
        send(c, OWN, 0, rows, to_right, 1)
        send(c, OWN, 0, rows, partner, 6)
        pair(c, OWN)

    def take_x(c):
        wait(c, XP, 0, rows, 0)
        send(c, XP, 0, half, to_left, 2)
        wait(c, XM, 0, rows, 1)
        send(c, XM, half, half, to_right, 3)
        if ROWS_X[c] < rows:
            send(c, XP, ROWS_X[c], rows - ROWS_X[c], partner, 8)
            send(c, XM, ROWS_X[c], rows - ROWS_X[c], partner, 9)
        pair(c, XP)
        pair(c, XM)

    def take_z(c):
        wait(c, ZO, 0, rows, 6)
        pair(c, ZO)

    def pieces(c):
        size = ROWS_X[c] // PIECES[c]
        return [(i * size, size) for i in range(PIECES[c])]

    def send_far(c):
        for i, (first, count) in enumerate(pieces(c)):
            send(c, ZO, first, count, to_left, (4, 10)[i])
            send(c, ZO, first, count, to_right, (5, 11)[i])

    def take_halves(c):
        wait(c, X2, 0, half, 2)
        wait(c, X2, half, half, 3)
        send(c, X2, 0, rows, partner, 7)
        pair(c, X2)

    def take_far(c):
        if ROWS_X[c] < rows:
            wait(c, PP, ROWS_X[c], rows - ROWS_X[c], 8)
            wait(c, PM, ROWS_X[c], rows - ROWS_X[c], 9)
        for i, (first, count) in enumerate(pieces(c)):
            on = rows - first if i == PIECES[c] - 1 else count
            wait(c, PP, first, count, (4, 10)[i])
            send(c, PP, first, on, sibling, (LANE + 5, 12)[i])
            wait(c, PM, first, count, (5, 11)[i])
            send(c, PM, first, on, sibling, (LANE + 6, 13)[i])

    def sibling_pieces(c, pos):
        slot = LANE + ALL.index(pos)
        if pos not in (PP, PM) or PIECES[c] == 1:
            return [(0, rows, slot)]
        size = ROWS_X[c] // PIECES[c]
        return [(0, size, slot), (size, rows - size, 12 if pos == PP else 13)]

    def take_corner(c):
        wait(c, CO, 0, rows, 7)
        pair(c, CO)

    started = set()

    def first_column(pos):
        return pl.multiple_of((lax.rem(zh + pos[0], 2) * 4 + lax.rem(x + pos[1], 4)) * 2 * rows, 1024)

    def project(c, names):
        positions = [BY_NAME[name] for name in names]
        for pos in positions:
            for first, count, slot in sibling_pieces(c, pos):
                wait(c, pos, first, count, slot, dc=1)
        columns = slice(0, w[c].shape[1])
        fresh = c not in started
        started.add(c)

        def multiply():
            total = None if fresh else acc[c % 2, :, columns]
            for pos in positions:
                at = pl.ds(first_column(pos), 2 * rows)
                part_sum = jnp.dot(tok[:, at], w[c][at], preferred_element_type=jnp.float32)
                total = part_sum if total is None else total + part_sum
            acc[c % 2, :, columns] = total

        apart(multiply)

    def project_part(c, name, dc):
        pos = BY_NAME[name]
        if dc == 1:
            for first, count, slot in sibling_pieces(c, pos):
                wait(c, pos, first, count, slot, dc=1)
        columns = slice(0, w[c].shape[1])
        at = pl.ds(pl.multiple_of(device(pos[0], pos[1], dc) * rows, 512), rows)

        def multiply():
            acc[c % 2, :, columns] += jnp.dot(tok[:, at], w[c][at], preferred_element_type=jnp.float32)

        apart(multiply)

    def round_chunk(c):
        def rounded():
            for h in range(CHUNKS[c][1]):
                qkv[CHUNKS[c][0] + h] = acc[c % 2, :, h * HEAD:(h + 1) * HEAD].astype(jnp.bfloat16)

        apart(rounded)

    def attend(c, ids):
        first, count = CHUNKS[c]
        tiles = tokens // TILE

        def tile_pair(i):
            work = [(first + h, i) for h in range(2)] if count == 2 else [(first, i), (first, tiles - 1 - i)]
            scores = [lax.dot_general(qkv[h, j * TILE:(j + 1) * TILE], qkv[0, :(j + 1) * TILE], (((1,), (1,)), ((), ())),
                                      preferred_element_type=jnp.float32)
                      + bias[j * TILE:(j + 1) * TILE, :(j + 1) * TILE] for h, j in work]
            weights = [jnp.exp2((s - jnp.max(s, axis=1, keepdims=True)) * EXP2_SCALE) for s in scores]
            for (h, j), p in zip(work, weights):
                total = jnp.sum(p, axis=1, keepdims=True)
                o = jnp.dot(p.astype(jnp.bfloat16), qkv[1, :(j + 1) * TILE], preferred_element_type=jnp.float32)
                out[j * TILE:(j + 1) * TILE, (h - 2) * HEAD:(h - 1) * HEAD] = (o / total).astype(jnp.bfloat16)

        def all_pairs():
            for i in ids:
                tile_pair(i)

        apart(all_pairs)

    def loads(c):
        at = pl.ds(pl.multiple_of(me * rows, rows), rows)
        if c == 0:
            return [pltpu.make_async_copy(wk_hbm, w[0].at[at, pl.ds(0, HEAD)], load_sem.at[0]),
                    pltpu.make_async_copy(wv_hbm, w[0].at[at, pl.ds(HEAD, HEAD)], load_sem.at[len(CHUNKS)])]
        first, count = CHUNKS[c]
        return [pltpu.make_async_copy(
            wq_hbm.at[:, pl.ds((first - 2) * HEAD, count * HEAD)], w[c].at[at], load_sem.at[c])]

    def tok_copy(name):
        at = pl.ds(first_column(BY_NAME[name]), 2 * rows)
        return pltpu.make_async_copy(tok_hbm.at[:, at], tok.at[:, at], tok_sem.at[ALL.index(BY_NAME[name])])

    for copy in loads(0):
        copy.start()

    barrier = pltpu.get_barrier_semaphore()
    for target in (to_left, to_right, partner, sibling):
        pl.semaphore_signal(barrier, inc=1, device_id=target, device_id_type=MESH)
    for c in range(1, len(CHUNKS)):
        for copy in loads(c):
            copy.start()
    pl.semaphore_wait(barrier, 4)

    begun = 0
    while ORDER[begun][0] == "own":
        for copy in loads(ORDER[begun][1]):
            copy.wait()
        send_own(ORDER[begun][1])
        begun += 1
    for c in range(begun, len(CHUNKS)):
        for copy in loads(c):
            copy.wait()
    seg_copy = pltpu.make_async_copy(seg_hbm, seg_ref, seg_sem)
    seg_copy.start()
    for name in BY_NAME:
        tok_copy(name).start()
    seg_copy.wait()

    def fill_mask():
        for i in range(tokens // HEAD):
            mine = jnp.transpose(jnp.broadcast_to(seg_ref[i:i + 1, :], (HEAD, HEAD)))
            for j in range((i * HEAD // TILE + 1) * TILE // HEAD):
                ok = mine == jnp.broadcast_to(seg_ref[j:j + 1, :], (HEAD, HEAD))
                t = lax.broadcasted_iota(jnp.int32, (HEAD, HEAD), 0) + i * HEAD
                u = lax.broadcasted_iota(jnp.int32, (HEAD, HEAD), 1) + j * HEAD
                bias[i * HEAD:(i + 1) * HEAD, j * HEAD:(j + 1) * HEAD] = jnp.where(
                    jnp.logical_and(ok, u <= t), jnp.float32(0.0), jnp.float32(NEGATIVE))

    apart(fill_mask)

    def drain(c):
        far = pieces(c) + [(0, 0)]
        rest = rows - ROWS_X[c]
        on = [sibling_pieces(c, pos) for pos in ALL]
        for slot, (pos, first, count) in enumerate(
                [(OWN, 0, rows), (OWN, 0, rows), (XP, 0, half), (XM, half, half), (ZO,) + far[0], (ZO,) + far[0],
                 (OWN, 0, rows), (X2, 0, rows), (XP, ROWS_X[c], rest), (XM, ROWS_X[c], rest), (ZO,) + far[1], (ZO,) + far[1]]
                + [(pos,) + (on[ALL.index(pos)] + [(0, 0)])[1][:2] for pos in (PP, PM)]
                + [(pos,) + on[i][0][:2] for i, pos in enumerate(ALL)]):
            if count > 0:
                ref = part(c, pos, 0, first, count)
                pltpu.make_async_remote_copy(
                    src_ref=ref, dst_ref=ref, send_sem=send_sem.at[c, slot], recv_sem=recv_sem.at[c, slot],
                    device_id=sibling, device_id_type=MESH).wait_send()

    steps = dict(own=send_own, x=take_x, z=take_z, far=send_far, halves=take_halves, take_far=take_far, corner=take_corner,
                 mul=project, part=project_part, round=round_chunk, attend=attend)
    runs = []
    for step in ORDER[begun:]:
        if len(step) != 3:
            runs.append(step)
        elif runs and runs[-1][:2] == step[:2] and (
                len(runs[-1][2]) < MUL_RUN if step[0] == "mul" else sum(i + 1 for i in runs[-1][2]) + step[2] < TILE_RUN):
            runs[-1][2].append(step[2])
        else:
            runs.append((step[0], step[1], [step[2]]))
    seen = set()
    drained = False
    for run in runs:
        if run[1] == last and run[0] in ("take_far", "corner") and not drained:
            for c in range(last):
                drain(c)
            drained = True
        if run[0] == "mul":
            for name in run[2]:
                if name not in seen:
                    tok_copy(name).wait()
                    seen.add(name)
        steps[run[0]](*run[1:])

    drain(last)


def body(tokens, w_query, key_weight, value_weight, segment_ids):
    seq, width = tokens.shape
    columns = w_query.shape[1]
    heads = columns // HEAD
    any_space = pl.BlockSpec(memory_space=pl.ANY)
    in_vmem = pl.BlockSpec(memory_space=pltpu.VMEM)
    return pl.pallas_call(
        kernel,
        out_shape=pltpu.VMEM((seq, columns), jnp.bfloat16),
        in_specs=[any_space] * 5,
        out_specs=in_vmem,
        scratch_shapes=[
            pltpu.VMEM((seq, width), jnp.bfloat16),
            pltpu.VMEM((2, seq, 2 * HEAD), jnp.float32),
            pltpu.VMEM((heads + 2, seq, HEAD), jnp.bfloat16),
            pltpu.VMEM((seq, seq), jnp.float32),
            pltpu.VMEM((seq // HEAD, HEAD), jnp.int32),
            pltpu.SemaphoreType.DMA((len(CHUNKS) + 1,)),
            pltpu.SemaphoreType.DMA((8,)),
            pltpu.SemaphoreType.DMA,
            pltpu.SemaphoreType.DMA((len(CHUNKS), LANE + BLOCKS)),
            pltpu.SemaphoreType.DMA((len(CHUNKS), LANE + BLOCKS)),
        ] + [pltpu.VMEM((width, count * HEAD), jnp.bfloat16) for _, count in CHUNKS],
        compiler_params=pltpu.CompilerParams(
            collective_id=0, has_side_effects=True, vmem_limit_bytes=58 * 2**20),
        cost_estimate=pl.CostEstimate(
            flops=2 * seq * width * (columns + 2 * HEAD), bytes_accessed=40 * 2**20, transcendentals=heads * seq * seq),
    )(tokens, w_query, key_weight, value_weight, segment_ids.reshape(seq // HEAD, HEAD))


def solution(mesh):
    in_specs = (P("dp", None), P("dp", "head"), P("dp", "head"), P("dp", "head"), P("dp"))
    return jax.shard_map(body, mesh=mesh, in_specs=in_specs, out_specs=P("dp", "head"), check_vma=False)
```

```python
import functools
import math

import jax
import jax.numpy as jnp
from jax import lax
from jax.experimental import pallas as pl
from jax.experimental.pallas import tpu as pltpu
from jax.sharding import PartitionSpec as P

MESH = pl.DeviceIdType.MESH
HEAD = 128
NEGATIVE = -1e30
EXP2_SCALE = math.log2(math.e) / math.sqrt(HEAD)
LANE = 14
BLOCKS = 8
ROWS_X = (368, 400, 448, 384, 480)
PIECES = (1, 1, 1, 1, 1)
MUL_RUN = 2
TILE_RUN = 4
TILE = 256

CHUNKS = ((0, 2), (2, 2), (4, 2), (6, 2), (8, 2))

ORDER = (
    ("own", 0), ("own", 1), ("z", 0), ("x", 0), ("far", 0), ("own", 2), ("z", 1), ("take_far", 0),
    ("halves", 0), ("x", 1), ("x", 2), ("mul", 0, "XM"), ("corner", 0), ("z", 2), ("mul", 1, "ZO"),
    ("mul", 0, "PP"), ("halves", 1), ("far", 1), ("far", 2), ("mul", 1, "XP"), ("mul", 0, "XP"),
    ("mul", 0, "CO"), ("halves", 2), ("mul", 1, "XM"), ("mul", 0, "PM"), ("mul", 1, "OWN"), ("mul", 0, "OWN"),
    ("take_far", 1), ("mul", 0, "X2"), ("own", 3), ("mul", 0, "ZO"), ("round", 0), ("own", 4),
    ("mul", 2, "XP"), ("corner", 1), ("mul", 1, "X2"), ("mul", 2, "X2"), ("mul", 2, "XM"), ("take_far", 2),
    ("mul", 2, "OWN"), ("mul", 1, "PP"), ("mul", 1, "CO"), ("mul", 2, "PM"), ("mul", 1, "PM"), ("corner", 2),
    ("mul", 2, "PP"), ("round", 1), ("x", 3), ("mul", 2, "CO"), ("attend", 1, 2), ("mul", 2, "ZO"),
    ("attend", 1, 3), ("round", 2), ("attend", 1, 0), ("attend", 2, 3), ("attend", 1, 1), ("z", 3), ("far", 3),
    ("attend", 2, 1), ("attend", 2, 0), ("mul", 4, "OWN"), ("mul", 3, "OWN"), ("halves", 3), ("z", 4),
    ("x", 4), ("mul", 3, "XM"), ("far", 4), ("mul", 3, "ZO"), ("mul", 3, "XP"), ("attend", 2, 2),
    ("mul", 4, "ZO"), ("take_far", 3), ("mul", 3, "X2"), ("mul", 4, "XP"), ("mul", 4, "XM"), ("halves", 4),
    ("mul", 3, "PP"), ("corner", 3), ("mul", 3, "PM"), ("mul", 4, "X2"), ("mul", 3, "CO"), ("round", 3),
    ("attend", 3, 0), ("attend", 3, 1), ("attend", 3, 2), ("take_far", 4), ("attend", 3, 3),
    ("part", 4, "PP", 0), ("corner", 4), ("part", 4, "CO", 0), ("part", 4, "PM", 0), ("part", 4, "PP", 1),
    ("part", 4, "PM", 1), ("part", 4, "CO", 1), ("round", 4), ("attend", 4, 1), ("attend", 4, 3),
    ("attend", 4, 2), ("attend", 4, 0),
)


def kernel(tok_hbm, wq_hbm, wk_hbm, wv_hbm, seg_hbm, out, tok, acc, qkv, bias, seg_ref,
           load_sem, tok_sem, seg_sem, send_sem, recv_sem, *w):
    tokens = tok.shape[0]
    rows = wq_hbm.shape[0]
    half = rows // 2
    last = len(CHUNKS) - 1
    me = lax.axis_index("dp")
    head = lax.axis_index("head")
    zh, x, core = me // 8, lax.rem(me // 2, 4), lax.rem(me, 2)

    def device(dz, dx, dc):
        return (lax.rem(zh + dz, 2) * 4 + lax.rem(x + dx, 4)) * 2 + lax.rem(core + dc, 2)

    OWN, XP, XM, X2, ZO, PP, PM, CO = (0, 0), (0, 1), (0, 3), (0, 2), (1, 0), (1, 1), (1, 3), (1, 2)
    ALL = (OWN, XP, XM, X2, ZO, PP, PM, CO)
    BY_NAME = dict(OWN=OWN, XP=XP, XM=XM, X2=X2, ZO=ZO, PP=PP, PM=PM, CO=CO)
    to_left, to_right = (device(0, 3, 0), head), (device(0, 1, 0), head)
    partner, sibling = (device(1, 0, 0), head), (device(0, 0, 1), head)

    def apart(work):
        pl.when(me >= 0)(work)

    def part(c, pos, dc, first, count):
        start = pl.multiple_of(device(pos[0], pos[1], dc) * rows + first, 16)
        return w[c].at[pl.ds(start, count)]

    def send(c, pos, first, count, target, slot):
        ref = part(c, pos, 0, first, count)
        pltpu.make_async_remote_copy(
            src_ref=ref, dst_ref=ref, send_sem=send_sem.at[c, slot], recv_sem=recv_sem.at[c, slot],
            device_id=target, device_id_type=MESH).start()

    def pair(c, pos):
        send(c, pos, 0, rows, sibling, LANE + ALL.index(pos))

    def wait(c, pos, first, count, slot, dc=0):
        ref = part(c, pos, dc, first, count)
        pltpu.make_async_remote_copy(
            src_ref=ref, dst_ref=ref, send_sem=send_sem.at[c, slot], recv_sem=recv_sem.at[c, slot],
            device_id=sibling, device_id_type=MESH).wait_recv()

    def send_own(c):
        send(c, OWN, 0, rows, to_left, 0)
        send(c, OWN, 0, rows, to_right, 1)
        send(c, OWN, 0, rows, partner, 6)
        pair(c, OWN)

    def take_x(c):
        wait(c, XP, 0, rows, 0)
        send(c, XP, 0, half, to_left, 2)
        wait(c, XM, 0, rows, 1)
        send(c, XM, half, half, to_right, 3)
        if ROWS_X[c] < rows:
            send(c, XP, ROWS_X[c], rows - ROWS_X[c], partner, 8)
            send(c, XM, ROWS_X[c], rows - ROWS_X[c], partner, 9)
        pair(c, XP)
        pair(c, XM)

    def take_z(c):
        wait(c, ZO, 0, rows, 6)
        pair(c, ZO)

    def pieces(c):
        size = ROWS_X[c] // PIECES[c]
        return [(i * size, size) for i in range(PIECES[c])]

    def send_far(c):
        for i, (first, count) in enumerate(pieces(c)):
            send(c, ZO, first, count, to_left, (4, 10)[i])
            send(c, ZO, first, count, to_right, (5, 11)[i])

    def take_halves(c):
        wait(c, X2, 0, half, 2)
        wait(c, X2, half, half, 3)
        send(c, X2, 0, rows, partner, 7)
        pair(c, X2)

    def take_far(c):
        if ROWS_X[c] < rows:
            wait(c, PP, ROWS_X[c], rows - ROWS_X[c], 8)
            wait(c, PM, ROWS_X[c], rows - ROWS_X[c], 9)
        for i, (first, count) in enumerate(pieces(c)):
            on = rows - first if i == PIECES[c] - 1 else count
            wait(c, PP, first, count, (4, 10)[i])
            send(c, PP, first, on, sibling, (LANE + 5, 12)[i])
            wait(c, PM, first, count, (5, 11)[i])
            send(c, PM, first, on, sibling, (LANE + 6, 13)[i])

    def sibling_pieces(c, pos):
        slot = LANE + ALL.index(pos)
        if pos not in (PP, PM) or PIECES[c] == 1:
            return [(0, rows, slot)]
        size = ROWS_X[c] // PIECES[c]
        return [(0, size, slot), (size, rows - size, 12 if pos == PP else 13)]

    def take_corner(c):
        wait(c, CO, 0, rows, 7)
        pair(c, CO)

    started = set()

    def first_column(pos):
        return pl.multiple_of((lax.rem(zh + pos[0], 2) * 4 + lax.rem(x + pos[1], 4)) * 2 * rows, 1024)

    def project(c, names):
        positions = [BY_NAME[name] for name in names]
        for pos in positions:
            for first, count, slot in sibling_pieces(c, pos):
                wait(c, pos, first, count, slot, dc=1)
        columns = slice(0, w[c].shape[1])
        fresh = c not in started
        started.add(c)

        def multiply():
            total = None if fresh else acc[c % 2, :, columns]
            for pos in positions:
                at = pl.ds(first_column(pos), 2 * rows)
                part_sum = jnp.dot(tok[:, at], w[c][at], preferred_element_type=jnp.float32)
                total = part_sum if total is None else total + part_sum
            acc[c % 2, :, columns] = total

        apart(multiply)

    def project_part(c, name, dc):
        pos = BY_NAME[name]
        if dc == 1:
            for first, count, slot in sibling_pieces(c, pos):
                wait(c, pos, first, count, slot, dc=1)
        columns = slice(0, w[c].shape[1])
        at = pl.ds(pl.multiple_of(device(pos[0], pos[1], dc) * rows, 512), rows)

        def multiply():
            acc[c % 2, :, columns] += jnp.dot(tok[:, at], w[c][at], preferred_element_type=jnp.float32)

        apart(multiply)

    def round_chunk(c):
        def rounded():
            for h in range(CHUNKS[c][1]):
                qkv[CHUNKS[c][0] + h] = acc[c % 2, :, h * HEAD:(h + 1) * HEAD].astype(jnp.bfloat16)

        apart(rounded)

    def attend(c, ids):
        first, count = CHUNKS[c]
        tiles = tokens // TILE

        def tile_pair(i):
            work = [(first + h, i) for h in range(2)] if count == 2 else [(first, i), (first, tiles - 1 - i)]
            scores = [lax.dot_general(qkv[h, j * TILE:(j + 1) * TILE], qkv[0, :(j + 1) * TILE], (((1,), (1,)), ((), ())),
                                      preferred_element_type=jnp.float32)
                      + bias[j * TILE:(j + 1) * TILE, :(j + 1) * TILE] for h, j in work]
            weights = [jnp.exp2((s - jnp.max(s, axis=1, keepdims=True)) * EXP2_SCALE) for s in scores]
            for (h, j), p in zip(work, weights):
                total = jnp.sum(p, axis=1, keepdims=True)
                o = jnp.dot(p.astype(jnp.bfloat16), qkv[1, :(j + 1) * TILE], preferred_element_type=jnp.float32)
                out[j * TILE:(j + 1) * TILE, (h - 2) * HEAD:(h - 1) * HEAD] = (o / total).astype(jnp.bfloat16)

        def all_pairs():
            for i in ids:
                tile_pair(i)

        apart(all_pairs)

    def loads(c):
        at = pl.ds(pl.multiple_of(me * rows, rows), rows)
        if c == 0:
            return [pltpu.make_async_copy(wk_hbm, w[0].at[at, pl.ds(0, HEAD)], load_sem.at[0]),
                    pltpu.make_async_copy(wv_hbm, w[0].at[at, pl.ds(HEAD, HEAD)], load_sem.at[len(CHUNKS)])]
        first, count = CHUNKS[c]
        return [pltpu.make_async_copy(
            wq_hbm.at[:, pl.ds((first - 2) * HEAD, count * HEAD)], w[c].at[at], load_sem.at[c])]

    def tok_copy(name):
        at = pl.ds(first_column(BY_NAME[name]), 2 * rows)
        return pltpu.make_async_copy(tok_hbm.at[:, at], tok.at[:, at], tok_sem.at[ALL.index(BY_NAME[name])])

    for copy in loads(0):
        copy.start()

    barrier = pltpu.get_barrier_semaphore()
    for target in (to_left, to_right, partner, sibling):
        pl.semaphore_signal(barrier, inc=1, device_id=target, device_id_type=MESH)
    for c in range(1, len(CHUNKS)):
        for copy in loads(c):
            copy.start()
    pl.semaphore_wait(barrier, 4)

    begun = 0
    while ORDER[begun][0] == "own":
        for copy in loads(ORDER[begun][1]):
            copy.wait()
        send_own(ORDER[begun][1])
        begun += 1
    for c in range(begun, len(CHUNKS)):
        for copy in loads(c):
            copy.wait()
    seg_copy = pltpu.make_async_copy(seg_hbm, seg_ref, seg_sem)
    seg_copy.start()
    for name in BY_NAME:
        tok_copy(name).start()
    seg_copy.wait()

    def fill_mask():
        for i in range(tokens // HEAD):
            mine = jnp.transpose(jnp.broadcast_to(seg_ref[i:i + 1, :], (HEAD, HEAD)))
            for j in range((i * HEAD // TILE + 1) * TILE // HEAD):
                ok = mine == jnp.broadcast_to(seg_ref[j:j + 1, :], (HEAD, HEAD))
                t = lax.broadcasted_iota(jnp.int32, (HEAD, HEAD), 0) + i * HEAD
                u = lax.broadcasted_iota(jnp.int32, (HEAD, HEAD), 1) + j * HEAD
                bias[i * HEAD:(i + 1) * HEAD, j * HEAD:(j + 1) * HEAD] = jnp.where(
                    jnp.logical_and(ok, u <= t), jnp.float32(0.0), jnp.float32(NEGATIVE))

    apart(fill_mask)

    def drain(c):
        far = pieces(c) + [(0, 0)]
        rest = rows - ROWS_X[c]
        on = [sibling_pieces(c, pos) for pos in ALL]
        for slot, (pos, first, count) in enumerate(
                [(OWN, 0, rows), (OWN, 0, rows), (XP, 0, half), (XM, half, half), (ZO,) + far[0], (ZO,) + far[0],
                 (OWN, 0, rows), (X2, 0, rows), (XP, ROWS_X[c], rest), (XM, ROWS_X[c], rest), (ZO,) + far[1], (ZO,) + far[1]]
                + [(pos,) + (on[ALL.index(pos)] + [(0, 0)])[1][:2] for pos in (PP, PM)]
                + [(pos,) + on[i][0][:2] for i, pos in enumerate(ALL)]):
            if count > 0:
                ref = part(c, pos, 0, first, count)
                pltpu.make_async_remote_copy(
                    src_ref=ref, dst_ref=ref, send_sem=send_sem.at[c, slot], recv_sem=recv_sem.at[c, slot],
                    device_id=sibling, device_id_type=MESH).wait_send()

    steps = dict(own=send_own, x=take_x, z=take_z, far=send_far, halves=take_halves, take_far=take_far, corner=take_corner,
                 mul=project, part=project_part, round=round_chunk, attend=attend)
    runs = []
    for step in ORDER[begun:]:
        if len(step) != 3:
            runs.append(step)
        elif runs and runs[-1][:2] == step[:2] and (
                len(runs[-1][2]) < MUL_RUN if step[0] == "mul" else sum(i + 1 for i in runs[-1][2]) + step[2] < TILE_RUN):
            runs[-1][2].append(step[2])
        else:
            runs.append((step[0], step[1], [step[2]]))
    seen = set()
    drained = False
    parts_left = sum(run[0] == "part" for run in runs)
    for run in runs:
        if run[0] == "part":
            parts_left -= 1
            if parts_left == 0:
                drain(last)
        if run[1] == last and run[0] in ("take_far", "corner") and not drained:
            for c in range(last):
                drain(c)
            drained = True
        if run[0] == "mul":
            for name in run[2]:
                if name not in seen:
                    tok_copy(name).wait()
                    seen.add(name)
        steps[run[0]](*run[1:])


def body(tokens, w_query, key_weight, value_weight, segment_ids):
    seq, width = tokens.shape
    columns = w_query.shape[1]
    heads = columns // HEAD
    any_space = pl.BlockSpec(memory_space=pl.ANY)
    in_vmem = pl.BlockSpec(memory_space=pltpu.VMEM)
    return pl.pallas_call(
        kernel,
        out_shape=pltpu.VMEM((seq, columns), jnp.bfloat16),
        in_specs=[any_space] * 5,
        out_specs=in_vmem,
        scratch_shapes=[
            pltpu.VMEM((seq, width), jnp.bfloat16),
            pltpu.VMEM((2, seq, 2 * HEAD), jnp.float32),
            pltpu.VMEM((heads + 2, seq, HEAD), jnp.bfloat16),
            pltpu.VMEM((seq, seq), jnp.float32),
            pltpu.VMEM((seq // HEAD, HEAD), jnp.int32),
            pltpu.SemaphoreType.DMA((len(CHUNKS) + 1,)),
            pltpu.SemaphoreType.DMA((8,)),
            pltpu.SemaphoreType.DMA,
            pltpu.SemaphoreType.DMA((len(CHUNKS), LANE + BLOCKS)),
            pltpu.SemaphoreType.DMA((len(CHUNKS), LANE + BLOCKS)),
        ] + [pltpu.VMEM((width, count * HEAD), jnp.bfloat16) for _, count in CHUNKS],
        compiler_params=pltpu.CompilerParams(
            collective_id=0, has_side_effects=True, vmem_limit_bytes=58 * 2**20),
        cost_estimate=pl.CostEstimate(
            flops=2 * seq * width * (columns + 2 * HEAD), bytes_accessed=40 * 2**20, transcendentals=heads * seq * seq),
    )(tokens, w_query, key_weight, value_weight, segment_ids.reshape(seq // HEAD, HEAD))


def solution(mesh):
    in_specs = (P("dp", None), P("dp", "head"), P("dp", "head"), P("dp", "head"), P("dp"))
    return jax.shard_map(body, mesh=mesh, in_specs=in_specs, out_specs=P("dp", "head"), check_vma=False)
```
